256 devices in a mesh: seq: 32 (over z, x), res: 8 (over y, core).
Axes of the slice: x: 4, y: 4, z: 8, core: 2. Of those that a mesh axis runs over, the one named last changes fastest.
Arguments:
- alignment_rows: float32 [128, 1024, 768], P('seq', 'res'), may hold values from -5 to 5
- query_matrix: bfloat16 [768, 768], replicated, may hold values from -1 to 1
- key_matrix: bfloat16 [768, 768], replicated, may hold values from -1 to 1
- value_matrix: bfloat16 [768, 768], replicated, may hold values from -0.21875 to 0.21875
- output_matrix: bfloat16 [768, 768], replicated, may hold values from -1.5 to 1.5
Outputs:
- attended_rows: float32 [128, 1024, 768], P('seq', 'res')
The draws below stay inside these ranges and needn't reach their ends.
All inputs are finite; a program needn't handle non-finite values.
Results may differ from the reference program's by a relative error of at most 0.012.
Values may be sent and summed in bfloat16 or wider, within the bound.
A program may use at most 128 MiB of HBM per device.

```python
import math
import jax
import jax.numpy as jnp
from jax import lax

D = 768
HEADS = 12
HEAD_DIM = 64
SEQS = 128
RESIDUES = 1024


def shared_base(key):
    return jnp.clip(jax.random.normal(key, (D, D), jnp.float32), -4.0, 4.0) / math.sqrt(D)


def draw_query_matrix(key, part):
    base = shared_base(key)
    return (2.0 * base).astype(jnp.bfloat16)


def draw_key_matrix(key, part):
    key = jax.random.fold_in(key, 12)
    own = jnp.clip(jax.random.normal(key, (D, D), jnp.float32), -4.0, 4.0) / math.sqrt(D)
    mixed = own
    return mixed.astype(jnp.bfloat16)


def draw_alignment_rows(key, part):
    key = jax.random.fold_in(key, 13)
    noise = jnp.clip(jax.random.normal(key, (SEQS, RESIDUES, D), jnp.float32), -5.0, 5.0)
    result = noise
    return jnp.clip(result, -5.0, 5.0).astype(jnp.float32)


def gaussian(own_key, shape, deviation, limit, dtype=jnp.bfloat16):
    return jnp.clip(deviation * jax.random.normal(own_key, shape, jnp.float32), -limit, limit).astype(dtype)


def setup_inputs(seed: int = 0) -> dict:
    arg_keys = jax.random.split(jax.random.key(seed), 6)
    return {
        "alignment_rows": draw_alignment_rows(jax.random.fold_in(arg_keys[5], 71), 0),
        "query_matrix": draw_query_matrix(jax.random.fold_in(arg_keys[5], 71), 0),
        "key_matrix": draw_key_matrix(jax.random.fold_in(arg_keys[5], 71), 0),
        "value_matrix": gaussian(arg_keys[3], (D, D), D ** -0.5, 0.21875),
        "output_matrix": gaussian(arg_keys[4], (D, D), 0.108, 1.5),
    }


epsilon = 1e-05

def layer_normalize(values):
    mean_val = lax.optimization_barrier(jnp.mean(values, axis=-1, keepdims=True))
    centred = values - mean_val
    spread = lax.optimization_barrier(jnp.mean(centred * centred, axis=-1, keepdims=True))
    return centred * lax.rsqrt(spread + epsilon)

def reference(alignment_rows, query_matrix, key_matrix, value_matrix, output_matrix):
    sequence_total, residue_total, hidden_width = alignment_rows.shape
    normalized_rows = layer_normalize(alignment_rows).astype(jnp.bfloat16).reshape(sequence_total * residue_total, hidden_width)

    def project(weight):
        full = jnp.dot(normalized_rows, weight, preferred_element_type=jnp.float32).astype(jnp.bfloat16)
        return jnp.moveaxis(full.reshape(sequence_total, residue_total, HEADS, HEAD_DIM), 2, 0)
    queries = project(query_matrix)
    keys_all = project(key_matrix)
    values_all = project(value_matrix)
    scale_val = 1.0 / math.sqrt(HEAD_DIM * sequence_total)

    def one_head(triple):
        query_h, key_h, value_h = triple
        scores = jnp.einsum('sid,sjd->ij', query_h.astype(jnp.float32), key_h.astype(jnp.float32)) * scale_val
        peak_val = lax.optimization_barrier(jnp.max(scores, axis=1, keepdims=True))
        expo = jnp.exp(scores - peak_val)
        weights_bf = (expo / lax.optimization_barrier(jnp.sum(expo, axis=1, keepdims=True))).astype(jnp.bfloat16)
        return jnp.einsum('ij,sjd->sid', weights_bf.astype(jnp.float32), value_h.astype(jnp.float32))
    heads_out = lax.map(one_head, (queries, keys_all, values_all))
    mixed = jnp.moveaxis(heads_out, 0, 2).astype(jnp.bfloat16).reshape(sequence_total * residue_total, hidden_width)
    result = jnp.dot(mixed, output_matrix, preferred_element_type=jnp.float32)
    return result.reshape(sequence_total, residue_total, hidden_width)
```

```python
import math

import jax
import jax.numpy as jnp
from jax import lax
from jax.experimental import pallas as pl
from jax.experimental.pallas import tpu as pltpu
from jax.sharding import PartitionSpec as P

MESH = pl.DeviceIdType.MESH
F32 = jnp.float32
BF16 = jnp.bfloat16

NZ, NX, NY = 8, 4, 4
CHUNKS = 3
SEQ_LOCAL, RES_LOCAL, WIDTH = 4, 128, 768
ROWS = NY * RES_LOCAL
COLS = 2 * ROWS
DEPTH = 256
SCALE = 1.0 / math.sqrt(64 * 128)
EPSILON = 1e-05
N_SEMS = 128


def kernel(
    x_hbm, wq_hbm, wk_hbm, wv_hbm, wo_hbm, o_ref,
    x_v, n_v, w_v, wo_v, send_v, q_v, k_v, v_v, sc_v, p_v,
    rx1, rxl, rxr, tmp, xs_v, rz, rzr, rzl, tz, zs_v, rx, os_v, ob_v, m_v,
    load_sem, ss, rs,
):
    s_id, r_id = lax.axis_index("seq"), lax.axis_index("res")
    z, x = s_id // NX, s_id % NX
    y, core = r_id // 2, r_id % 2

    def dev(dz=0, dx=0, dy=0, dc=0):
        return (
            ((z + dz) % NZ) * NX + (x + dx) % NX,
            ((y + dy) % NY) * 2 + (core + dc) % 2,
        )

    partners = (
        [dict(dy=d) for d in (1, 2, 3)]
        + [dict(dc=1)]
        + [dict(dx=d) for d in (1, 2, 3)]
        + [dict(dz=d) for d in range(1, 8)]
    )

    loads = {}
    n_load = [0]

    def load(name, src, dst):
        c = pltpu.make_async_copy(src, dst, load_sem.at[n_load[0]])
        n_load[0] += 1
        c.start()
        loads[name] = c

    for s in range(SEQ_LOCAL):
        load(("x", s), x_hbm.at[s], x_v.at[s])
    w_hbm = (wq_hbm, wk_hbm, wv_hbm)
    for t in (0, 1):
        load(("w", t, 0), w_hbm[t].at[:, pl.ds(0, DEPTH)], w_v.at[t, 0])
    for c in (1, 2):
        for t in (0, 1):
            load(("w", t, c), w_hbm[t].at[:, pl.ds(c * DEPTH, DEPTH)], w_v.at[t, c])
    for c in range(CHUNKS):
        load(("w", 2, c), w_hbm[2].at[:, pl.ds(c * DEPTH, DEPTH)], w_v.at[2, c])
    load("wo", wo_hbm, wo_v)

    barrier = pltpu.get_barrier_semaphore()
    for p in partners:
        pl.semaphore_signal(barrier, inc=1, device_id=dev(**p), device_id_type=MESH)

    count = [0]
    started = []

    def send(src, dst, **where):
        i = count[0]
        count[0] += 1
        c = pltpu.make_async_remote_copy(
            src_ref=src, dst_ref=dst, send_sem=ss.at[i], recv_sem=rs.at[i],
            device_id=dev(**where), device_id_type=MESH,
        )
        c.start()
        started.append(c)
        return c

    for s in range(SEQ_LOCAL):
        loads[("x", s)].wait()
        v = x_v[s]
        mean = jnp.mean(v, axis=-1, keepdims=True)
        cen = v - mean
        var = jnp.mean(cen * cen, axis=-1, keepdims=True)
        n_v[pl.ds(s * RES_LOCAL, RES_LOCAL), :] = (cen * lax.rsqrt(var + EPSILON)).astype(BF16)

    def swap(blocks, j):
        return jnp.concatenate([b[:, 64 * j : 64 * j + 64] for b in blocks], axis=1)

    def project(t, c):
        loads[("w", t, c)].wait()
        full = jnp.dot(n_v[...], w_v[t, c], preferred_element_type=F32).astype(BF16)
        blocks = [full[s * RES_LOCAL : (s + 1) * RES_LOCAL] for s in range(SEQ_LOCAL)]
        for j in range(NY):
            send_v[t, c, j] = swap(blocks, j)

    homes = (q_v, None, None)

    def home(t, c):
        if t == 0:
            return q_v.at[c]
        return (k_v if t == 1 else v_v).at[c, 0]

    def send_y(t, c):
        out = []
        for d in (1, 2, 3):
            out.append(send(send_v.at[t, c, (y + d) % NY], home(t, c).at[y], dy=d))
        return out

    def keep(t, c):
        home(t, c)[y] = send_v[t, c, y]

    def core_swap(t, c):
        b = (k_v if t == 1 else v_v)
        return send(b.at[c, 0], b.at[c, 1], dc=1)

    def scores(c):
        q = q_v[c].reshape(ROWS, DEPTH)

        def step(n, carry):
            half, part = n // 2, n % 2
            k = k_v[c, half, pl.ds(part * 2, 2)].reshape(2 * RES_LOCAL, DEPTH)
            r = lax.dot_general(q, k, (((1,), (1,)), ((), ())), preferred_element_type=F32)
            sc_v[c, :, pl.ds(pl.multiple_of(n * 256, 256), 256)] = (r * SCALE).astype(BF16)
            return carry

        lax.fori_loop(0, 4, step, 0)

    def rows(ref, off, n):
        return ref[pl.ds(pl.multiple_of(off, 16), n), :].astype(F32)

    def at(ref, off, n):
        return ref.at[pl.ds(pl.multiple_of(off, 16), n)]

    xr, xl, xo = (x + 1) % NX, (x + 3) % NX, (x + 2) % NX

    def softmax16(v):
        peak = jnp.max(v, axis=-1, keepdims=True)
        e = jnp.exp(v - peak)
        return (e / jnp.sum(e, axis=-1, keepdims=True)).astype(BF16)

    def xfirst(c, g):
        sc = sc_v.at[c]
        pv = p_v.at[c]
        st = {}

        def start():
            st["r1"] = send(at(sc, xo * 128, 64), rx1.at[g, 0], dx=1)
            st["l1"] = send(at(sc, xo * 128 + 64, 64), rx1.at[g, 1], dx=3)
            st["r2"] = send(at(sc, xr * 128 + 64, 64), rxl.at[g, pl.ds(64, 64)], dx=1)
            st["l2"] = send(at(sc, xl * 128, 64), rxr.at[g, pl.ds(0, 64)], dx=3)

        def relay():
            st["r1"].wait_recv()
            tmp[g, 0] = (rows(sc, xr * 128, 64) + rx1[g, 0].astype(F32)).astype(BF16)
            st["r3"] = send(tmp.at[g, 0], rxl.at[g, pl.ds(0, 64)], dx=1)
            st["l1"].wait_recv()
            tmp[g, 1] = (rows(sc, xl * 128 + 64, 64) + rx1[g, 1].astype(F32)).astype(BF16)
            st["l3"] = send(tmp.at[g, 1], rxr.at[g, pl.ds(64, 64)], dx=3)

        def zsend():
            for k in ("r2", "l2", "r3", "l3"):
                st[k].wait_recv()
            total = rows(sc, x * 128, 128) + rxl[g].astype(F32) + rxr[g].astype(F32)
            xs_v[g] = total.astype(BF16).reshape(NZ, 16, COLS)
            st["z"] = [
                send(xs_v.at[g, (z + d) % NZ], rz.at[g, d - 1], dz=d) for d in range(1, 8)
            ]

        def finish():
            own = z * 16
            total = rows(sc, x * 128 + own, 16)
            total = total + rows(rxl.at[g], own, 16) + rows(rxr.at[g], own, 16)
            for d in range(7):
                st["z"][d].wait_recv()
                total = total + rz[g, d].astype(F32)
            mine = at(pv, x * 128 + own, 16)
            mine[...] = softmax16(total)
            st["za"] = [send(mine, mine, dz=d) for d in range(1, 8)]

        def xgather():
            for k in st["za"]:
                k.wait_recv()
            block = at(pv, x * 128, 128)
            st["ra"] = send(block, block, dx=1)
            st["la"] = send(block, block, dx=3)

        def xforward():
            st["ra"].wait_recv()
            block = at(pv, xl * 128, 64)
            st["rb"] = send(block, block, dx=1)
            st["la"].wait_recv()
            block = at(pv, xr * 128 + 64, 64)
            st["lb"] = send(block, block, dx=3)

        def done():
            st["rb"].wait_recv()
            st["lb"].wait_recv()

        return [start, relay, zsend, finish, xgather, xforward, done]

    def zfirst(c):
        sc = sc_v.at[c]
        pv = p_v.at[c]
        st = {}

        def ring(k):
            def go():
                if k == 1:
                    st["r"] = send(at(sc, ((z + 4) % NZ) * 64, 32), rzr.at[0, pl.ds(0, 32)], dz=1)
                    st["l"] = send(at(sc, ((z + 4) % NZ) * 64 + 32, 32), rzl.at[0, pl.ds(32, 32)], dz=7)
                    return
                dr, dl = (z + 5 - k) % NZ, (z + 3 + k) % NZ
                st["r"].wait_recv()
                if k == 2:
                    tz[0, 0, pl.ds(0, 32), :] = (
                        rows(sc, dr * 64, 32) + rzr[0, pl.ds(0, 32), :].astype(F32)
                    ).astype(BF16)
                    tz[0, 0, pl.ds(32, 32), :] = sc[pl.ds(pl.multiple_of(dr * 64 + 32, 32), 32), :]
                else:
                    tz[k - 2, 0] = (rows(sc, dr * 64, 64) + rzr[k - 2].astype(F32)).astype(BF16)
                st["r"] = send(tz.at[k - 2, 0], rzr.at[k - 1], dz=1)
                st["l"].wait_recv()
                if k == 2:
                    tz[0, 1, pl.ds(32, 32), :] = (
                        rows(sc, dl * 64 + 32, 32) + rzl[0, pl.ds(32, 32), :].astype(F32)
                    ).astype(BF16)
                    tz[0, 1, pl.ds(0, 32), :] = sc[pl.ds(pl.multiple_of(dl * 64, 32), 32), :]
                else:
                    tz[k - 2, 1] = (rows(sc, dl * 64, 64) + rzl[k - 2].astype(F32)).astype(BF16)
                st["l"] = send(tz.at[k - 2, 1], rzl.at[k - 1], dz=7)

            return go

        def xsend():
            st["r"].wait_recv()
            st["l"].wait_recv()
            zs_v[...] = (
                rows(sc, z * 64, 64) + rzr[3].astype(F32) + rzl[3].astype(F32)
            ).reshape(NX, 16, COLS)
            st["x"] = [send(zs_v.at[(x + d) % NX], rx.at[d - 1], dx=d) for d in (1, 2, 3)]

        def finish():
            total = zs_v[x]
            for d in range(3):
                st["x"][d].wait_recv()
                total = total + rx[d]
            mine = at(pv, z * 64 + x * 16, 16)
            mine[...] = softmax16(total)
            st["xa"] = [send(mine, mine, dx=d) for d in (1, 2, 3)]

        def gather(k):
            def go():
                if k == 1:
                    for cp in st["xa"]:
                        cp.wait_recv()
                    b = at(pv, z * 64, 64)
                    st["gr"] = send(b, b, dz=1)
                    st["gl"] = send(b, b, dz=7)
                    return
                zr, zl = (z + k - 1) % NZ, (z + 9 - k) % NZ
                st["gr"].wait_recv()
                b = at(pv, zl * 64, 64 if k < 4 else 32)
                st["gr"] = send(b, b, dz=1)
                st["gl"].wait_recv()
                b = at(pv, zr * 64, 64) if k < 4 else at(pv, zr * 64 + 32, 32)
                st["gl"] = send(b, b, dz=7)

            return go

        def done():
            st["gr"].wait_recv()
            st["gl"].wait_recv()

        return [ring(1), ring(2), ring(3), ring(4), xsend, finish, gather(1), gather(2), gather(3), gather(4), done]

    def mix(c):
        v = v_v[c].reshape(COLS, DEPTH)

        def step(i, carry):
            m = jnp.dot(
                p_v[c, pl.ds(pl.multiple_of(i * 256, 256), 256), :], v, preferred_element_type=F32
            ).astype(BF16)
            os_v[c, pl.ds(i * 2, 2)] = m.reshape(2, RES_LOCAL, DEPTH)
            return carry

        lax.fori_loop(0, 2, step, 0)
        ob_v[c, y] = os_v[c, y]
        return [send(os_v.at[c, (y + d) % NY], ob_v.at[c, y], dy=d) for d in (1, 2, 3)]

    def output(c, first):
        blocks = [ob_v[c, j] for j in range(NY)]
        for s in range(SEQ_LOCAL):
            m_v[pl.ds(s * RES_LOCAL, RES_LOCAL), :] = swap(blocks, s)

        def step(n, carry):
            cols = pl.ds(pl.multiple_of(n * 256, 256), 256)
            r = jnp.dot(
                m_v[...], wo_v[pl.ds(c * DEPTH, DEPTH), cols], preferred_element_type=F32
            )
            if first:
                o_ref[:, cols] = r
            else:
                o_ref[:, cols] += r
            return carry

        lax.fori_loop(0, 3, step, 0)

    def wait_all(cps):
        for cp in cps:
            cp.wait_recv()

    project(0, 0)
    project(1, 0)
    pl.semaphore_wait(barrier, len(partners))
    qk = {}
    qk[0] = send_y(1, 0) + send_y(0, 0)
    keep(0, 0), keep(1, 0)
    for c in (1, 2):
        project(0, c), project(1, c)
        keep(0, c), keep(1, c)
    h0 = xfirst(0, 0)
    h1 = zfirst(1)
    h2 = xfirst(2, 1)

    def take(c):
        wait_all(qk[c][:3])
        kc = core_swap(1, c)
        wait_all(qk[c][3:])
        if c < 2:
            qk[c + 1] = send_y(1, c + 1) + send_y(0, c + 1)
        kc.wait_recv()
        scores(c)

    take(0)
    h0[0]()
    for c in range(CHUNKS):
        project(2, c)
        keep(2, c)
    h0[1]()
    take(1)
    h1[0]()
    h1[1]()
    h0[2]()
    h1[2]()
    take(2)
    vs = [send_y(2, c) for c in range(CHUNKS)]
    h2[0]()
    h1[3]()
    h2[1]()
    h0[3]()
    h1[4]()
    h2[2]()
    h0[4]()
    h1[5]()
    h1[6]()
    h2[3]()
    h0[5]()
    h1[7]()
    vc = []
    for c in range(CHUNKS):
        wait_all(vs[c])
        vc.append(core_swap(2, c))
    h2[4]()
    h1[8]()
    h1[9]()
    loads["wo"].wait()
    h0[6]()
    vc[0].wait_recv()
    o0 = mix(0)
    h2[5]()
    h1[10]()
    vc[1].wait_recv()
    o1 = mix(1)
    wait_all(o0)
    output(0, True)
    wait_all(o1)
    output(1, False)
    h2[6]()
    vc[2].wait_recv()
    o2 = mix(2)
    wait_all(o2)
    output(2, False)
    for cp in started:
        cp.wait_send()


def body(alignment_rows, query_matrix, key_matrix, value_matrix, output_matrix):
    any_spec = pl.BlockSpec(memory_space=pl.ANY)
    V = pltpu.VMEM
    out = pl.pallas_call(
        kernel,
        out_shape=jax.ShapeDtypeStruct((SEQ_LOCAL * RES_LOCAL, WIDTH), F32),
        in_specs=[any_spec] * 5,
        out_specs=pl.BlockSpec(memory_space=V),
        scratch_shapes=[
            V((SEQ_LOCAL, RES_LOCAL, WIDTH), F32),
            V((SEQ_LOCAL * RES_LOCAL, WIDTH), BF16),
            V((3, CHUNKS, WIDTH, DEPTH), BF16),
            V((WIDTH, WIDTH), BF16),
            V((3, CHUNKS, NY, RES_LOCAL, DEPTH), BF16),
            V((CHUNKS, NY, RES_LOCAL, DEPTH), BF16),
            V((CHUNKS, 2, NY, RES_LOCAL, DEPTH), BF16),
            V((CHUNKS, 2, NY, RES_LOCAL, DEPTH), BF16),
            V((CHUNKS, ROWS, COLS), BF16),
            V((CHUNKS, ROWS, COLS), BF16),
            V((2, 2, 64, COLS), BF16),
            V((2, 128, COLS), BF16),
            V((2, 128, COLS), BF16),
            V((2, 2, 64, COLS), BF16),
            V((2, NZ, 16, COLS), BF16),
            V((2, 7, 16, COLS), BF16),
            V((4, 64, COLS), BF16),
            V((4, 64, COLS), BF16),
            V((3, 2, 64, COLS), BF16),
            V((NX, 16, COLS), F32),
            V((3, 16, COLS), F32),
            V((CHUNKS, NY, RES_LOCAL, DEPTH), BF16),
            V((CHUNKS, NY, RES_LOCAL, DEPTH), BF16),
            V((SEQ_LOCAL * RES_LOCAL, DEPTH), BF16),
            pltpu.SemaphoreType.DMA((16,)),
            pltpu.SemaphoreType.DMA((N_SEMS,)),
            pltpu.SemaphoreType.DMA((N_SEMS,)),
        ],
        compiler_params=pltpu.CompilerParams(
            collective_id=0, has_side_effects=True, vmem_limit_bytes=56 << 20
        ),
        cost_estimate=pl.CostEstimate(
            flops=9_000_000_000, bytes_accessed=8_000_000, transcendentals=60_000
        ),
    )(alignment_rows, query_matrix, key_matrix, value_matrix, output_matrix)
    return out.reshape(alignment_rows.shape)


def solution(mesh):
    in_specs = (P("seq", "res", None), P(), P(), P(), P())
    out_specs = P("seq", "res", None)
    return jax.shard_map(body, mesh=mesh, in_specs=in_specs, out_specs=out_specs, check_vma=False)
```

```python
import math

import jax
import jax.numpy as jnp
from jax import lax
from jax.experimental import pallas as pl
from jax.experimental.pallas import tpu as pltpu
from jax.sharding import PartitionSpec as P

MESH = pl.DeviceIdType.MESH
F32 = jnp.float32
BF16 = jnp.bfloat16

NZ, NX, NY = 8, 4, 4
CHUNKS = 3
SEQ_LOCAL, RES_LOCAL, WIDTH = 4, 128, 768
ROWS = NY * RES_LOCAL
COLS = 2 * ROWS
DEPTH = 256
SCALE = 1.0 / math.sqrt(64 * 128)
EPSILON = 1e-05
N_SEMS = 216

GROUPS = (("x", 768), ("z", 256),)


def kernel(x_hbm, wq_hbm, wk_hbm, wv_hbm, o_ref, *scratch):
    (x_v, n_v, w_v, send_v, q_v, k_v, v_v, os_v, ob_v, m_v, load_sem, ss, rs) = scratch[:13]
    group_refs, at = [], 13
    for kind, _ in GROUPS:
        size = 8 if kind == "x" else 7
        group_refs.append(scratch[at : at + size])
        at += size
    s_id, r_id = lax.axis_index("seq"), lax.axis_index("res")
    z, x = s_id // NX, s_id % NX
    y, core = r_id // 2, r_id % 2

    def dev(dz=0, dx=0, dy=0, dc=0):
        return (
            ((z + dz) % NZ) * NX + (x + dx) % NX,
            ((y + dy) % NY) * 2 + (core + dc) % 2,
        )

    partners = (
        [dict(dy=d) for d in (1, 2, 3)]
        + [dict(dc=1)]
        + [dict(dx=d) for d in (1, 2, 3)]
        + [dict(dz=d) for d in range(1, 8)]
    )

    loads = {}
    n_load = [0]

    def load(name, src, dst):
        c = pltpu.make_async_copy(src, dst, load_sem.at[n_load[0]])
        n_load[0] += 1
        c.start()
        loads[name] = c

    for s in range(SEQ_LOCAL):
        load(("x", s), x_hbm.at[s], x_v.at[s])
    w_hbm = (wq_hbm, wk_hbm, wv_hbm)
    for t in (0, 1):
        load(("w", t, 0), w_hbm[t].at[:, pl.ds(0, DEPTH)], w_v.at[t, 0])
    for c in (1, 2):
        for t in (0, 1):
            load(("w", t, c), w_hbm[t].at[:, pl.ds(c * DEPTH, DEPTH)], w_v.at[t, c])
    for c in range(CHUNKS):
        load(("w", 2, c), w_hbm[2].at[:, pl.ds(c * DEPTH, DEPTH)], w_v.at[2, c])

    barrier = pltpu.get_barrier_semaphore()
    for p in partners:
        pl.semaphore_signal(barrier, inc=1, device_id=dev(**p), device_id_type=MESH)

    count = [0]
    started = []

    def send(src, dst, **where):
        i = count[0]
        count[0] += 1
        c = pltpu.make_async_remote_copy(
            src_ref=src, dst_ref=dst, send_sem=ss.at[i], recv_sem=rs.at[i],
            device_id=dev(**where), device_id_type=MESH,
        )
        c.start()
        started.append(c)
        return c

    for s in range(SEQ_LOCAL):
        loads[("x", s)].wait()
        v = x_v[s]
        mean = jnp.mean(v, axis=-1, keepdims=True)
        cen = v - mean
        var = jnp.mean(cen * cen, axis=-1, keepdims=True)
        n_v[pl.ds(s * RES_LOCAL, RES_LOCAL), :] = (cen * lax.rsqrt(var + EPSILON)).astype(BF16)

    def swap(blocks, j):
        return jnp.concatenate([b[:, 64 * j : 64 * j + 64] for b in blocks], axis=1)

    def project(t, c):
        loads[("w", t, c)].wait()
        full = jnp.dot(n_v[...], w_v[t, c], preferred_element_type=F32).astype(BF16)
        blocks = [full[s * RES_LOCAL : (s + 1) * RES_LOCAL] for s in range(SEQ_LOCAL)]
        for j in range(NY):
            send_v[t, c, j] = swap(blocks, j)

    def home(t, c):
        if t == 0:
            return q_v.at[c]
        return (k_v if t == 1 else v_v).at[c, 0]

    def send_y(t, c):
        out = []
        for d in (1, 2, 3):
            out.append(send(send_v.at[t, c, (y + d) % NY], home(t, c).at[y], dy=d))
        return out

    def keep(t, c):
        home(t, c)[y] = send_v[t, c, y]

    def core_swap(t, c):
        b = (k_v if t == 1 else v_v)
        return send(b.at[c, 0], b.at[c, 1], dc=1)

    starts = [sum(w for _, w in GROUPS[:g]) for g in range(len(GROUPS))]

    def scores(c, g):
        kind, w = GROUPS[g]
        q = q_v[c].reshape(ROWS, DEPTH)
        k = k_v[c].reshape(COLS, DEPTH)[starts[g] : starts[g] + w]
        r = lax.dot_general(q, k, (((1,), (1,)), ((), ())), preferred_element_type=F32)
        r = (r * SCALE).astype(BF16)
        s_v = group_refs[g][0]
        if kind == "x":
            s_v[c] = r.reshape(NX, NZ, 16, w)
        else:
            for i in range(NX):
                s_v[c, :, i] = r[i * 128 : (i + 1) * 128].reshape(NZ, 16, w)

    xr, xl, xo = (x + 1) % NX, (x + 3) % NX, (x + 2) % NX
    lo, hi = pl.ds(0, 4), pl.ds(4, 4)

    def wide(v):
        return v.astype(F32)

    class AlongX:
        def __init__(self, c, refs):
            s_v, p_v, self.rx1, self.rxl, self.rxr, self.tmp, self.xs, self.rz = (r.at[c] for r in refs)
            self.s, self.p = s_v, p_v

        def start(self):
            s = self.s
            self.r1 = send(s.at[xo, lo], self.rx1.at[0], dx=1)
            self.l1 = send(s.at[xo, hi], self.rx1.at[1], dx=3)
            self.r2 = send(s.at[xr, hi], self.rxl.at[hi], dx=1)
            self.l2 = send(s.at[xl, lo], self.rxr.at[lo], dx=3)

        def relay(self):
            s = self.s
            self.r1.wait_recv()
            self.tmp[0] = (wide(s[xr, lo]) + wide(self.rx1[0])).astype(BF16)
            self.r3 = send(self.tmp.at[0], self.rxl.at[lo], dx=1)
            self.l1.wait_recv()
            self.tmp[1] = (wide(s[xl, hi]) + wide(self.rx1[1])).astype(BF16)
            self.l3 = send(self.tmp.at[1], self.rxr.at[hi], dx=3)

        def total(self):
            for cp in (self.r2, self.l2, self.r3, self.l3):
                cp.wait_recv()
            self.xs[...] = (wide(self.s[x]) + wide(self.rxl[...]) + wide(self.rxr[...])).astype(BF16)
            self.z = [
                send(self.xs.at[(z + d) % NZ], self.rz.at[d - 1], dz=d) for d in (4, 3, 5, 2, 6, 1, 7)
            ]

        def final(self):
            v = wide(self.s[x, z]) + wide(self.rxl[z]) + wide(self.rxr[z])
            wait_all(self.z)
            for d in range(7):
                v = v + wide(self.rz[d])
            return v

        def put(self, p):
            self.p[x, z] = p
            mine = self.p.at[x, z]
            self.g = [send(mine, mine, dz=d) for d in (4, 3, 5, 2, 6, 1, 7)]

        def gather(self):
            wait_all(self.g)
            b = self.p.at[x]
            self.ra, self.la = send(b, b, dx=1), send(b, b, dx=3)

        def forward(self):
            self.ra.wait_recv()
            b = self.p.at[xl, lo]
            self.rb = send(b, b, dx=1)
            self.la.wait_recv()
            b = self.p.at[xr, hi]
            self.lb = send(b, b, dx=3)

        def done(self):
            wait_all((self.rb, self.lb))

        def rows(self, i):
            return self.p[i].reshape(128, self.p.shape[-1])

    class AlongZ:
        def __init__(self, c, refs):
            s_v, p_v, self.zr, self.zl, self.tz, self.zs, self.rx = (r.at[c] for r in refs)
            self.s, self.p = s_v, p_v

        def start(self):
            o = (z + 4) % NZ
            self.r = send(self.s.at[o, pl.ds(0, 2)], self.zr.at[0, pl.ds(0, 2)], dz=1)
            self.l = send(self.s.at[o, pl.ds(2, 2)], self.zl.at[0, pl.ds(2, 2)], dz=7)

        def ring(self, k):
            s, tz = self.s, self.tz
            dr, dl = (z + 5 - k) % NZ, (z + 3 + k) % NZ
            self.r.wait_recv()
            if k == 2:
                tz[0, 0, pl.ds(0, 2)] = (
                    wide(s[dr, pl.ds(0, 2)]) + wide(self.zr[0, pl.ds(0, 2)])
                ).astype(BF16)
                tz[0, 0, pl.ds(2, 2)] = s[dr, pl.ds(2, 2)]
            else:
                tz[k - 2, 0] = (wide(s[dr]) + wide(self.zr[k - 2])).astype(BF16)
            self.r = send(tz.at[k - 2, 0], self.zr.at[k - 1], dz=1)
            self.l.wait_recv()
            if k == 2:
                tz[0, 1, pl.ds(2, 2)] = (
                    wide(s[dl, pl.ds(2, 2)]) + wide(self.zl[0, pl.ds(2, 2)])
                ).astype(BF16)
                tz[0, 1, pl.ds(0, 2)] = s[dl, pl.ds(0, 2)]
            else:
                tz[k - 2, 1] = (wide(s[dl]) + wide(self.zl[k - 2])).astype(BF16)
            self.l = send(tz.at[k - 2, 1], self.zl.at[k - 1], dz=7)

        def total(self):
            self.r.wait_recv()
            self.l.wait_recv()
            self.zs[...] = wide(self.s[z]) + wide(self.zr[3]) + wide(self.zl[3])
            self.x = [send(self.zs.at[(x + d) % NX], self.rx.at[d - 1], dx=d) for d in (2, 1, 3)]

        def final(self):
            wait_all(self.x)
            return self.zs[x] + self.rx[0] + self.rx[1] + self.rx[2]

        def put(self, p):
            self.p[z, x] = p
            mine = self.p.at[z, x]
            self.g = [send(mine, mine, dx=d) for d in (2, 1, 3)]

        def gather(self, k):
            p = self.p
            if k == 1:
                wait_all(self.g)
                b = p.at[z]
                self.gr, self.gl = send(b, b, dz=1), send(b, b, dz=7)
                return
            zr, zl = (z + k - 1) % NZ, (z + 9 - k) % NZ
            self.gr.wait_recv()
            b = p.at[zl] if k < 4 else p.at[zl, pl.ds(0, 2)]
            self.gr = send(b, b, dz=1)
            self.gl.wait_recv()
            b = p.at[zr] if k < 4 else p.at[zr, pl.ds(2, 2)]
            self.gl = send(b, b, dz=7)

        def done(self):
            wait_all((self.gr, self.gl))

        def rows(self, i):
            return self.p[:, i].reshape(128, self.p.shape[-1])

    parts = [
        [(AlongX if kind == "x" else AlongZ)(c, refs) for (kind, _), refs in zip(GROUPS, group_refs)]
        for c in range(CHUNKS)
    ]
    by_axis = sorted(range(len(GROUPS)), key=lambda g: GROUPS[g][0] == "x")

    def soft(c):
        vals = {g: parts[c][g].final() for g in by_axis}
        peak = None
        for v in vals.values():
            m = jnp.max(v, axis=-1, keepdims=True)
            peak = m if peak is None else jnp.maximum(peak, m)
        total = 0.0
        for g in vals:
            vals[g] = jnp.exp(vals[g] - peak)
            total = total + jnp.sum(vals[g], axis=-1, keepdims=True)
        for g in vals:
            parts[c][g].put((vals[g] / total).astype(BF16))

    def mix(c):
        v = v_v[c].reshape(COLS, DEPTH)

        for i in (0, 2):
            m = None
            for g, (_, w) in enumerate(GROUPS):
                p = jnp.concatenate([parts[c][g].rows(i), parts[c][g].rows(i + 1)], axis=0)
                r = jnp.dot(p, v[starts[g] : starts[g] + w], preferred_element_type=F32)
                m = r if m is None else m + r
            os_v[c, pl.ds(i, 2)] = m.astype(BF16).reshape(2, RES_LOCAL, DEPTH)
        ob_v[c, y] = os_v[c, y]
        return [send(os_v.at[c, (y + d) % NY], ob_v.at[c, y], dy=d) for d in (1, 2, 3)]

    out_copies = []

    def output(c):
        blocks = [ob_v[c, j] for j in range(NY)]
        for s in range(SEQ_LOCAL):
            m_v[c, pl.ds(s * RES_LOCAL, RES_LOCAL), :] = swap(blocks, s)
        cp = pltpu.make_async_copy(
            m_v.at[c], o_ref.at[:, pl.ds(c * DEPTH, DEPTH)], load_sem.at[13 + c]
        )
        cp.start()
        out_copies.append(cp)

    def wait_all(cps):
        for cp in cps:
            cp.wait_recv()

    qk, vs, kc, vc, ms = {}, {}, {}, {}, {}

    def meet():
        pl.semaphore_wait(barrier, len(partners))

    def projections(c, ts):
        def go():
            for t in ts:
                project(t, c)
                keep(t, c)
        return go

    def qk_send(c):
        def go():
            qk[c] = send_y(1, c) + send_y(0, c)
        return go

    def k_swap(c):
        def go():
            wait_all(qk[c][:3])
            kc[c] = core_swap(1, c)
        return go

    def score(c):
        def go():
            wait_all(qk[c][3:])
            kc[c].wait_recv()
            for g in by_axis:
                scores(c, g)
                parts[c][g].start()
        return go

    def do(c, g, what, *args):
        return lambda: getattr(parts[c][g], what)(*args)

    def softmax(c):
        return lambda: soft(c)

    def v_send(c):
        def go():
            vs[c] = send_y(2, c)
        return go

    def v_swap(c):
        def go():
            wait_all(vs[c])
            vc[c] = core_swap(2, c)
        return go

    def mixing(c):
        def go():
            for p in parts[c]:
                p.done()
            vc[c].wait_recv()
            ms[c] = mix(c)
        return go

    def project_out(c):
        def go():
            wait_all(ms[c])
            output(c)
        return go

    schedule = [
        projections(0, (1, 0)), meet, qk_send(0), projections(1, (1, 0)), qk_send(1), projections(2, (1, 0)),
        qk_send(2), k_swap(0), score(0), do(0, 1, "ring", 2), k_swap(1), do(0, 0, "relay"),
        do(0, 1, "ring", 3), score(1), do(0, 1, "ring", 4), do(1, 1, "ring", 2), k_swap(2), do(0, 0, "total"),
        do(1, 0, "relay"), score(2), do(0, 1, "total"), do(1, 1, "ring", 3), projections(2, (2,)),
        do(2, 1, "ring", 2), do(1, 0, "total"), do(1, 1, "ring", 4), do(2, 0, "relay"), do(2, 1, "ring", 3),
        softmax(0), projections(0, (2,)), do(2, 1, "ring", 4), do(2, 0, "total"), do(1, 1, "total"),
        do(0, 1, "gather", 1), v_send(0), softmax(1), do(2, 1, "total"), do(0, 0, "gather"),
        projections(1, (2,)), softmax(2), v_send(1), do(0, 1, "gather", 2), do(1, 1, "gather", 1),
        do(0, 0, "forward"), do(1, 0, "gather"), do(2, 1, "gather", 1), v_send(2), do(0, 1, "gather", 3),
        v_swap(1), do(2, 0, "gather"), v_swap(0), do(1, 1, "gather", 2), do(2, 1, "gather", 2),
        do(0, 1, "gather", 4), do(1, 1, "gather", 3), do(1, 0, "forward"), do(2, 1, "gather", 3), mixing(0),
        do(1, 1, "gather", 4), do(2, 1, "gather", 4), do(2, 0, "forward"), v_swap(2), mixing(1), mixing(2),
        project_out(0), project_out(1), project_out(2),
    ]
    for step in schedule:
        step()
    for cp in out_copies:
        cp.wait()
    for cp in started:
        cp.wait_send()


def group_scratch(kind, w):
    V = pltpu.VMEM
    if kind == "x":
        shapes = [(NX, NZ, 16, w)] * 2 + [(2, 4, 16, w), (NZ, 16, w), (NZ, 16, w), (2, 4, 16, w), (NZ, 16, w), (7, 16, w)]
        return [V((CHUNKS,) + s, BF16) for s in shapes]
    shapes = [(NZ, NX, 16, w)] * 2 + [(4, NX, 16, w)] * 2 + [(3, 2, NX, 16, w)]
    return [V((CHUNKS,) + s, BF16) for s in shapes] + [V((CHUNKS, n, 16, w), F32) for n in (NX, 3)]


def body(alignment_rows, query_matrix, key_matrix, value_matrix, output_matrix):
    any_spec = pl.BlockSpec(memory_space=pl.ANY)
    V = pltpu.VMEM
    rows = SEQ_LOCAL * RES_LOCAL
    block = (NY, RES_LOCAL, DEPTH)
    scratch = [
        V((SEQ_LOCAL, RES_LOCAL, WIDTH), F32),
        V((rows, WIDTH), BF16),
        V((3, CHUNKS, WIDTH, DEPTH), BF16),
        V((3, CHUNKS) + block, BF16),
        V((CHUNKS,) + block, BF16),
        V((CHUNKS, 2) + block, BF16),
        V((CHUNKS, 2) + block, BF16),
        V((CHUNKS,) + block, BF16),
        V((CHUNKS,) + block, BF16),
        V((CHUNKS, rows, DEPTH), BF16),
        pltpu.SemaphoreType.DMA((16,)),
        pltpu.SemaphoreType.DMA((N_SEMS,)),
        pltpu.SemaphoreType.DMA((N_SEMS,)),
    ]
    for kind, w in GROUPS:
        scratch += group_scratch(kind, w)
    mixed = pl.pallas_call(
        kernel,
        out_shape=jax.ShapeDtypeStruct((rows, WIDTH), BF16),
        in_specs=[any_spec] * 4,
        out_specs=any_spec,
        scratch_shapes=scratch,
        compiler_params=pltpu.CompilerParams(
            collective_id=0, has_side_effects=True, vmem_limit_bytes=56 << 20
        ),
        cost_estimate=pl.CostEstimate(
            flops=5_000_000_000, bytes_accessed=6_000_000, transcendentals=60_000
        ),
    )(alignment_rows, query_matrix, key_matrix, value_matrix)
    out = jnp.dot(mixed, output_matrix, preferred_element_type=F32)
    return out.reshape(alignment_rows.shape)


def solution(mesh):
    in_specs = (P("seq", "res", None), P(), P(), P(), P())
    out_specs = P("seq", "res", None)
    return jax.shard_map(body, mesh=mesh, in_specs=in_specs, out_specs=out_specs, check_vma=False)
```

```python
import math

import jax
import jax.numpy as jnp
from jax import lax
from jax.experimental import pallas as pl
from jax.experimental.pallas import tpu as pltpu
from jax.sharding import PartitionSpec as P

MESH = pl.DeviceIdType.MESH
F32 = jnp.float32
BF16 = jnp.bfloat16

NZ, NX, NY = 8, 4, 4
CHUNKS = 3
SEQ_LOCAL, RES_LOCAL, WIDTH = 4, 128, 768
ROWS = NY * RES_LOCAL
COLS = 2 * ROWS
DEPTH = 256
SCALE = 1.0 / math.sqrt(64 * 128)
EPSILON = 1e-05
N_SEMS = 242

SUMS = (
    (("x", 640), ("z", 384),),
    (("x", 640), ("z", 384),),
    (("x", 640), ("z", 384),),
)
SPREADS = (
    (("x", 640), ("z", 384),),
    (("x", 640), ("z", 384),),
    (("x", 640), ("z", 384),),
)


def kernel(x_hbm, wq_hbm, wk_hbm, wv_hbm, o_ref, *scratch):
    (x_v, n_v, w_v, send_v, q_v, k_v, v_v, os_v, ob_v, m_v, load_sem, ss, rs) = scratch[:13]
    at = 13
    sum_refs, spread_refs = [], []
    for table, store, sizes in ((SUMS, sum_refs, {"x": 7, "z": 6}), (SPREADS, spread_refs, {"x": 1, "z": 1})):
        for row in table:
            store.append([])
            for kind, _ in row:
                store[-1].append(scratch[at : at + sizes[kind]])
                at += sizes[kind]
    s_id, r_id = lax.axis_index("seq"), lax.axis_index("res")
    z, chip_x = s_id // NX, s_id % NX
    y, core = r_id // 2, r_id % 2
    x = (chip_x + y) % NX

    def dev(dz=0, dx=0, dy=0, dc=0):
        return (
            ((z + dz) % NZ) * NX + (chip_x + dx) % NX,
            ((y + dy) % NY) * 2 + (core + dc) % 2,
        )

    partners = (
        [dict(dy=d) for d in (1, 2, 3)]
        + [dict(dc=1)]
        + [dict(dx=d) for d in (1, 2, 3)]
        + [dict(dz=d) for d in range(1, 8)]
    )

    loads = {}
    n_load = [0]

    def load(name, src, dst):
        c = pltpu.make_async_copy(src, dst, load_sem.at[n_load[0]])
        n_load[0] += 1
        c.start()
        loads[name] = c

    for s in range(SEQ_LOCAL):
        load(("x", s), x_hbm.at[s], x_v.at[s])
    w_hbm = (wq_hbm, wk_hbm, wv_hbm)
    for t in (0, 1):
        load(("w", t, 0), w_hbm[t].at[:, pl.ds(0, DEPTH)], w_v.at[t, 0])
    for c in (1, 2):
        for t in (0, 1):
            load(("w", t, c), w_hbm[t].at[:, pl.ds(c * DEPTH, DEPTH)], w_v.at[t, c])
    for c in range(CHUNKS):
        load(("w", 2, c), w_hbm[2].at[:, pl.ds(c * DEPTH, DEPTH)], w_v.at[2, c])

    barrier = pltpu.get_barrier_semaphore()
    for p in partners:
        pl.semaphore_signal(barrier, inc=1, device_id=dev(**p), device_id_type=MESH)

    count = [0]
    started = []

    def send(src, dst, **where):
        i = count[0]
        count[0] += 1
        c = pltpu.make_async_remote_copy(
            src_ref=src, dst_ref=dst, send_sem=ss.at[i], recv_sem=rs.at[i],
            device_id=dev(**where), device_id_type=MESH,
        )
        c.start()
        started.append(c)
        return c

    for s in range(SEQ_LOCAL):
        loads[("x", s)].wait()
        v = x_v[s]
        mean = jnp.mean(v, axis=-1, keepdims=True)
        cen = v - mean
        var = jnp.mean(cen * cen, axis=-1, keepdims=True)
        n_v[pl.ds(s * RES_LOCAL, RES_LOCAL), :] = (cen * lax.rsqrt(var + EPSILON)).astype(BF16)

    def swap(blocks, j):
        return jnp.concatenate([b[:, 64 * j : 64 * j + 64] for b in blocks], axis=1)

    def project(t, c):
        loads[("w", t, c)].wait()
        full = jnp.dot(n_v[...], w_v[t, c], preferred_element_type=F32).astype(BF16)
        blocks = [full[s * RES_LOCAL : (s + 1) * RES_LOCAL] for s in range(SEQ_LOCAL)]
        for j in range(NY):
            send_v[t, c, j] = swap(blocks, j)

    def home(t, c):
        if t == 0:
            return q_v.at[c]
        return (k_v if t == 1 else v_v).at[c, 0]

    def send_y(t, c):
        out = []
        for d in (1, 2, 3):
            out.append(send(send_v.at[t, c, (y + d) % NY], home(t, c).at[y], dy=d))
        return out

    def keep(t, c):
        home(t, c)[y] = send_v[t, c, y]

    def core_swap(t, c):
        b = (k_v if t == 1 else v_v)
        return send(b.at[c, 0], b.at[c, 1], dc=1)

    def starts(row):
        return [sum(w for _, w in row[:g]) for g in range(len(row))]

    def scores(c, g):
        kind, w = SUMS[c][g]
        first = starts(SUMS[c])[g]
        q = q_v[c].reshape(ROWS, DEPTH)
        k = k_v[c].reshape(COLS, DEPTH)[first : first + w]
        r = lax.dot_general(q, k, (((1,), (1,)), ((), ())), preferred_element_type=F32)
        r = (r * SCALE).astype(BF16)
        s_v = sum_refs[c][g][0]
        if kind == "x":
            s_v[...] = r.reshape(NX, NZ, 16, w)
        else:
            for i in range(NX):
                s_v[:, i] = r[i * 128 : (i + 1) * 128].reshape(NZ, 16, w)

    every = pl.ds(0, 16)

    def halves(w):
        first = w // 256 * 128
        return pl.ds(0, first), pl.ds(first, w - first)

    xr, xl, xo = (x + 1) % NX, (x + 3) % NX, (x + 2) % NX
    lo, hi = pl.ds(0, 4), pl.ds(4, 4)

    def wide(v):
        return v.astype(F32)

    class SumX:
        def __init__(self, refs):
            self.s, self.rx1, self.rxl, self.rxr, self.tmp, self.xs, self.zz = refs
            self.half = halves(self.s.shape[-1])

        def start(self):
            s = self.s
            self.r1 = send(s.at[xo, lo], self.rx1.at[0], dx=1)
            self.l1 = send(s.at[xo, hi], self.rx1.at[1], dx=3)
            self.r2 = send(s.at[xr, hi], self.rxl.at[hi], dx=1)
            self.l2 = send(s.at[xl, lo], self.rxr.at[lo], dx=3)

        def relay(self):
            s = self.s
            self.r1.wait_recv()
            self.tmp[0] = (wide(s[xr, lo]) + wide(self.rx1[0])).astype(BF16)
            self.r3 = send(self.tmp.at[0], self.rxl.at[lo], dx=1)
            self.l1.wait_recv()
            self.tmp[1] = (wide(s[xl, hi]) + wide(self.rx1[1])).astype(BF16)
            self.l3 = send(self.tmp.at[1], self.rxr.at[hi], dx=3)

        def total(self):
            for cp in (self.r2, self.l2, self.r3, self.l3):
                cp.wait_recv()
            self.xs[...] = (wide(self.s[x]) + wide(self.rxl[...]) + wide(self.rxr[...])).astype(BF16)
            xs, zz, (a, b) = self.xs, self.zz, self.half
            far = xs.at[(z + 4) % NZ]
            self.h = (send(far.at[every, a], zz.at[0, every, a], dz=2), send(far.at[every, b], zz.at[1, every, b], dz=6))
            self.t = (
                send(xs.at[(z + 3) % NZ], zz.at[2], dz=1),
                send(xs.at[(z + 5) % NZ], zz.at[3], dz=7),
            )
            self.d = (
                send(xs.at[(z + 1) % NZ], zz.at[4], dz=1),
                send(xs.at[(z + 7) % NZ], zz.at[5], dz=7),
            )

        def relay_z(self):
            zz = self.zz
            self.f = []
            for i in (0, 1):
                block = self.xs.at[(z + 2 + 4 * i) % NZ]
                wait_all((self.h[i], self.t[i]))
                near, far = self.half[1 - i], self.half[i]
                zz[6 + i, :, far] = (wide(block[:, far]) + wide(zz[2 + i, :, far]) + wide(zz[i, :, far])).astype(BF16)
                zz[6 + i, :, near] = (wide(block[:, near]) + wide(zz[2 + i, :, near])).astype(BF16)
                self.f.append(send(zz.at[6 + i], zz.at[8 + i], dz=2 + 4 * i))

        def final(self):
            v = wide(self.s[x, z]) + wide(self.rxl[z]) + wide(self.rxr[z])
            wait_all(self.d)
            wait_all(self.f)
            for k in (4, 5, 8, 9):
                v = v + wide(self.zz[k])
            return v

    class SumZ:
        def __init__(self, refs):
            self.s, self.zr, self.zl, self.tz, self.zs, self.rx = refs

        def start(self):
            o = (z + 4) % NZ
            self.r = send(self.s.at[o, pl.ds(0, 2)], self.zr.at[0, pl.ds(0, 2)], dz=1)
            self.l = send(self.s.at[o, pl.ds(2, 2)], self.zl.at[0, pl.ds(2, 2)], dz=7)

        def ring(self, k):
            s, tz = self.s, self.tz
            dr, dl = (z + 5 - k) % NZ, (z + 3 + k) % NZ
            self.r.wait_recv()
            if k == 2:
                tz[0, 0, pl.ds(0, 2)] = (
                    wide(s[dr, pl.ds(0, 2)]) + wide(self.zr[0, pl.ds(0, 2)])
                ).astype(BF16)
                tz[0, 0, pl.ds(2, 2)] = s[dr, pl.ds(2, 2)]
            else:
                tz[k - 2, 0] = (wide(s[dr]) + wide(self.zr[k - 2])).astype(BF16)
            self.r = send(tz.at[k - 2, 0], self.zr.at[k - 1], dz=1)
            self.l.wait_recv()
            if k == 2:
                tz[0, 1, pl.ds(2, 2)] = (
                    wide(s[dl, pl.ds(2, 2)]) + wide(self.zl[0, pl.ds(2, 2)])
                ).astype(BF16)
                tz[0, 1, pl.ds(0, 2)] = s[dl, pl.ds(0, 2)]
            else:
                tz[k - 2, 1] = (wide(s[dl]) + wide(self.zl[k - 2])).astype(BF16)
            self.l = send(tz.at[k - 2, 1], self.zl.at[k - 1], dz=7)

        def total(self):
            self.r.wait_recv()
            self.l.wait_recv()
            self.zs[...] = wide(self.s[z]) + wide(self.zr[3]) + wide(self.zl[3])
            self.x = [send(self.zs.at[(x + d) % NX], self.rx.at[d - 1], dx=d) for d in (2, 1, 3)]

        def final(self):
            wait_all(self.x)
            return self.zs[x] + self.rx[0] + self.rx[1] + self.rx[2]

    class SpreadX:
        def __init__(self, refs):
            (self.p,) = refs
            self.half = halves(self.p.shape[-1])

        def put(self, p):
            self.p[x, z] = p
            mine = self.p.at[x, z]
            self.two = (send(mine, mine, dz=2), send(mine, mine, dz=6))
            self.g = [send(mine, mine, dz=1), send(mine, mine, dz=7)]

        def pass_on(self):
            for i in (0, 1):
                self.two[i].wait_recv()
                block = self.p.at[x, (z + 6 - 4 * i) % NZ]
                half = block.at[every, self.half[i]]
                self.g.append(send(half, half, dz=2 + 4 * i))
                self.g.append(send(block, block, dz=1 + 6 * i))

        def gather(self):
            wait_all(self.g)
            b = self.p.at[x]
            self.ra, self.la = send(b, b, dx=1), send(b, b, dx=3)

        def forward(self):
            self.ra.wait_recv()
            b = self.p.at[xl, lo]
            self.rb = send(b, b, dx=1)
            self.la.wait_recv()
            b = self.p.at[xr, hi]
            self.lb = send(b, b, dx=3)

        def near(self):
            pass

        def done(self):
            wait_all((self.rb, self.lb))

        def rows(self, i):
            return self.p[i].reshape(128, self.p.shape[-1])

    class SpreadZ:
        def __init__(self, refs):
            (self.p,) = refs

        def put(self, p):
            self.p[z, x] = p
            mine = self.p.at[z, x]
            self.g = [send(mine, mine, dx=d) for d in (2, 1, 3)]

        def gather(self, k):
            p = self.p
            if k == 1:
                wait_all(self.g)
                b = p.at[z]
                self.gr, self.gl = send(b, b, dz=1), send(b, b, dz=7)
                return
            zr, zl = (z + k - 1) % NZ, (z + 9 - k) % NZ
            self.gr.wait_recv()
            b = p.at[zl] if k < 4 else p.at[zl, pl.ds(0, 2)]
            self.gr = send(b, b, dz=1)
            self.gl.wait_recv()
            b = p.at[zr] if k < 4 else p.at[zr, pl.ds(2, 2)]
            self.gl = send(b, b, dz=7)

        def near(self):
            wait_all((self.gr, self.gl))

        def done(self):
            pass

        def rows(self, i):
            return self.p[:, i].reshape(128, self.p.shape[-1])

    sums = [
        [(SumX if kind == "x" else SumZ)(refs) for (kind, _), refs in zip(SUMS[c], sum_refs[c])]
        for c in range(CHUNKS)
    ]
    spreads = [
        [
            (SpreadX if kind == "x" else SpreadZ)(refs)
            for (kind, _), refs in zip(SPREADS[c], spread_refs[c])
        ]
        for c in range(CHUNKS)
    ]

    def z_first(c):
        return sorted(range(len(SUMS[c])), key=lambda g: SUMS[c][g][0] == "x")

    def soft(c):
        vals = {g: sums[c][g].final() for g in z_first(c)}
        v = jnp.concatenate([vals[g] for g in range(len(vals))], axis=1)
        e = jnp.exp(v - jnp.max(v, axis=-1, keepdims=True))
        p = (e / jnp.sum(e, axis=-1, keepdims=True)).astype(BF16)
        for g, (_, w) in enumerate(SPREADS[c]):
            first = starts(SPREADS[c])[g]
            spreads[c][g].put(p[:, first : first + w])

    back = {}

    def mix_rows(c, i):
        v = v_v[c].reshape(COLS, DEPTH)
        m = None
        for g, (_, w) in enumerate(SPREADS[c]):
            first = starts(SPREADS[c])[g]
            r = jnp.dot(spreads[c][g].rows(i), v[first : first + w], preferred_element_type=F32)
            m = r if m is None else m + r
        os_v[c, i] = m.astype(BF16)
        d = (i - y + NY) % NY
        base = back[c]

        @pl.when(d == 0)
        def _():
            ob_v[c, y] = os_v[c, i]

        @pl.when(d != 0)
        def _():
            s_, r_ = dev()
            pltpu.make_async_remote_copy(
                src_ref=os_v.at[c, i], dst_ref=ob_v.at[c, y],
                send_sem=ss.at[base + d - 1], recv_sem=rs.at[base + d - 1],
                device_id=(s_, i * 2 + core), device_id_type=MESH,
            ).start()

    def mix_start(c):
        back[c] = count[0]
        count[0] += 3
        ms[c] = [
            pltpu.make_async_remote_copy(
                src_ref=os_v.at[c, (y + d) % NY], dst_ref=ob_v.at[c, y],
                send_sem=ss.at[back[c] + d - 1], recv_sem=rs.at[back[c] + d - 1],
                device_id=dev(dy=d), device_id_type=MESH,
            )
            for d in (1, 2, 3)
        ]
        started.extend(ms[c])

    out_copies = []

    def output(c):
        blocks = [ob_v[c, j] for j in range(NY)]
        for s in range(SEQ_LOCAL):
            m_v[c, pl.ds(s * RES_LOCAL, RES_LOCAL), :] = swap(blocks, s)
        cp = pltpu.make_async_copy(
            m_v.at[c], o_ref.at[:, pl.ds(c * DEPTH, DEPTH)], load_sem.at[13 + c]
        )
        cp.start()
        out_copies.append(cp)

    def wait_all(cps):
        for cp in cps:
            cp.wait_recv()

    qk, vs, kc, vc, ms = {}, {}, {}, {}, {}

    def meet():
        pl.semaphore_wait(barrier, len(partners))

    def projections(c, ts):
        def go():
            for t in ts:
                project(t, c)
                keep(t, c)
        return go

    def qk_send(c):
        def go():
            qk[c] = send_y(1, c) + send_y(0, c)
        return go

    def k_swap(c):
        def go():
            wait_all(qk[c][:3])
            kc[c] = core_swap(1, c)
        return go

    def score(c):
        def go():
            wait_all(qk[c][3:])
            kc[c].wait_recv()
            for g in z_first(c):
                scores(c, g)
                sums[c][g].start()
        return go

    def add(c, g, what, *args):
        return lambda: getattr(sums[c][g], what)(*args)

    def spread(c, g, what, *args):
        return lambda: getattr(spreads[c][g], what)(*args)

    def softmax(c):
        return lambda: soft(c)

    def v_send(c):
        def go():
            vs[c] = send_y(2, c)
        return go

    def v_swap(c):
        def go():
            wait_all(vs[c])
            vc[c] = core_swap(2, c)
        return go

    def mix_own(c):
        def go():
            for p in spreads[c]:
                p.near()
            vc[c].wait_recv()
            mix_start(c)
            mix_rows(c, x)
        return go

    def mix_near(c):
        def go():
            mix_rows(c, xl)
            mix_rows(c, xr)
        return go

    def mix_far(c):
        def go():
            for p in spreads[c]:
                p.done()
            mix_rows(c, xo)
        return go

    def project_out(c):
        def go():
            wait_all(ms[c])
            output(c)
        return go

    schedule = [
        projections(0, (1, 0)), meet, qk_send(0), projections(1, (1, 0)), projections(2, (1, 0)), qk_send(1),
        k_swap(0), score(0), qk_send(2), k_swap(1), add(0, 1, "ring", 2), projections(2, (2,)),
        add(0, 0, "relay"), score(1), projections(1, (2,)), add(0, 1, "ring", 3), k_swap(2),
        projections(0, (2,)), add(1, 1, "ring", 2), add(0, 0, "total"), add(1, 0, "relay"), score(2),
        add(0, 1, "ring", 4), add(1, 1, "ring", 3), v_send(0), v_send(1), add(0, 0, "relay_z"),
        add(2, 1, "ring", 2), add(1, 0, "total"), add(0, 1, "total"), add(2, 0, "relay"), add(1, 1, "ring", 4),
        add(2, 1, "ring", 3), add(1, 0, "relay_z"), softmax(0), add(1, 1, "total"), add(2, 0, "total"),
        add(2, 1, "ring", 4), spread(0, 1, "gather", 1), spread(0, 0, "pass_on"), v_send(2),
        add(2, 0, "relay_z"), v_swap(0), softmax(1), add(2, 1, "total"), spread(0, 1, "gather", 2),
        spread(0, 0, "gather"), spread(1, 1, "gather", 1), spread(1, 0, "pass_on"), softmax(2), v_swap(2),
        spread(0, 1, "gather", 3), spread(1, 1, "gather", 2), v_swap(1), spread(1, 0, "gather"),
        spread(2, 1, "gather", 1), spread(2, 0, "pass_on"), spread(0, 1, "gather", 4),
        spread(1, 1, "gather", 3), spread(2, 1, "gather", 2), spread(0, 0, "forward"), spread(2, 0, "gather"),
        mix_own(0), mix_near(0), spread(1, 1, "gather", 4), spread(1, 0, "forward"), spread(2, 1, "gather", 3),
        mix_far(0), mix_own(1), mix_near(1), spread(2, 1, "gather", 4), spread(2, 0, "forward"), mix_far(1),
        mix_own(2), mix_near(2), project_out(0), mix_far(2), project_out(1), project_out(2),
    ]
    for step in schedule:
        step()
    for cp in out_copies:
        cp.wait()
    for cp in started:
        cp.wait_send()


def sum_scratch(kind, w):
    V = pltpu.VMEM
    if kind == "x":
        shapes = [(NX, NZ, 16, w), (2, 4, 16, w), (NZ, 16, w), (NZ, 16, w), (2, 4, 16, w), (NZ, 16, w), (10, 16, w)]
        return [V(s, BF16) for s in shapes]
    shapes = [(NZ, NX, 16, w), (4, NX, 16, w), (4, NX, 16, w), (3, 2, NX, 16, w)]
    return [V(s, BF16) for s in shapes] + [V((n, 16, w), F32) for n in (NX, 3)]


def spread_scratch(kind, w):
    return [pltpu.VMEM((NZ, NX, 16, w) if kind == "z" else (NX, NZ, 16, w), BF16)]


def body(alignment_rows, query_matrix, key_matrix, value_matrix, output_matrix):
    any_spec = pl.BlockSpec(memory_space=pl.ANY)
    V = pltpu.VMEM
    rows = SEQ_LOCAL * RES_LOCAL
    block = (NY, RES_LOCAL, DEPTH)
    scratch = [
        V((SEQ_LOCAL, RES_LOCAL, WIDTH), F32),
        V((rows, WIDTH), BF16),
        V((3, CHUNKS, WIDTH, DEPTH), BF16),
        V((3, CHUNKS) + block, BF16),
        V((CHUNKS,) + block, BF16),
        V((CHUNKS, 2) + block, BF16),
        V((CHUNKS, 2) + block, BF16),
        V((CHUNKS,) + block, BF16),
        V((CHUNKS,) + block, BF16),
        V((CHUNKS, rows, DEPTH), BF16),
        pltpu.SemaphoreType.DMA((16,)),
        pltpu.SemaphoreType.DMA((N_SEMS,)),
        pltpu.SemaphoreType.DMA((N_SEMS,)),
    ]
    for table, make in ((SUMS, sum_scratch), (SPREADS, spread_scratch)):
        for row in table:
            for kind, w in row:
                scratch += make(kind, w)
    mixed = pl.pallas_call(
        kernel,
        out_shape=jax.ShapeDtypeStruct((rows, WIDTH), BF16),
        in_specs=[any_spec] * 4,
        out_specs=any_spec,
        scratch_shapes=scratch,
        compiler_params=pltpu.CompilerParams(
            collective_id=0, has_side_effects=True, vmem_limit_bytes=56 << 20
        ),
        cost_estimate=pl.CostEstimate(
            flops=5_000_000_000, bytes_accessed=6_000_000, transcendentals=60_000
        ),
    )(alignment_rows, query_matrix, key_matrix, value_matrix)
    out = jnp.dot(mixed, output_matrix, preferred_element_type=F32)
    return out.reshape(alignment_rows.shape)


def solution(mesh):
    in_specs = (P("seq", "res", None), P(), P(), P(), P())
    out_specs = P("seq", "res", None)
    return jax.shard_map(body, mesh=mesh, in_specs=in_specs, out_specs=out_specs, check_vma=False)
```

```python
import math

import jax
import jax.numpy as jnp
from jax import lax
from jax.experimental import pallas as pl
from jax.experimental.pallas import tpu as pltpu
from jax.sharding import PartitionSpec as P

MESH = pl.DeviceIdType.MESH
F32 = jnp.float32
BF16 = jnp.bfloat16

NZ, NX, NY = 8, 4, 4
CHUNKS = 3
SEQ_LOCAL, RES_LOCAL, WIDTH = 4, 128, 768
ROWS = NY * RES_LOCAL
COLS = 2 * ROWS
DEPTH = 256
SCALE = 1.0 / math.sqrt(64 * 128)
EPSILON = 1e-05
N_SEMS = 242

SUMS = (
    (("x", 640), ("z", 384),),
    (("x", 640), ("z", 384),),
    (("x", 640), ("z", 384),),
)
SPREADS = (
    (("x", 768), ("z", 256),),
    (("x", 640), ("z", 384),),
    (("x", 768), ("z", 256),),
)


def kernel(x_hbm, wq_hbm, wk_hbm, wv_hbm, o_ref, *scratch):
    (x_v, n_v, w_v, send_v, q_v, k_v, v_v, os_v, ob_v, m_v, load_sem, ss, rs) = scratch[:13]
    at = 13
    sum_refs, spread_refs = [], []
    for table, store, sizes in ((SUMS, sum_refs, {"x": 7, "z": 6}), (SPREADS, spread_refs, {"x": 1, "z": 1})):
        for row in table:
            store.append([])
            for kind, _ in row:
                store[-1].append(scratch[at : at + sizes[kind]])
                at += sizes[kind]
    s_id, r_id = lax.axis_index("seq"), lax.axis_index("res")
    z, chip_x = s_id // NX, s_id % NX
    y, core = r_id // 2, r_id % 2
    x = (chip_x + y) % NX

    def dev(dz=0, dx=0, dy=0, dc=0):
        return (
            ((z + dz) % NZ) * NX + (chip_x + dx) % NX,
            ((y + dy) % NY) * 2 + (core + dc) % 2,
        )

    partners = (
        [dict(dy=d) for d in (1, 2, 3)]
        + [dict(dc=1)]
        + [dict(dx=d) for d in (1, 2, 3)]
        + [dict(dz=d) for d in range(1, 8)]
    )

    loads = {}
    n_load = [0]

    def load(name, src, dst):
        c = pltpu.make_async_copy(src, dst, load_sem.at[n_load[0]])
        n_load[0] += 1
        c.start()
        loads[name] = c

    for s in range(SEQ_LOCAL):
        load(("x", s), x_hbm.at[s], x_v.at[s])
    w_hbm = (wq_hbm, wk_hbm, wv_hbm)
    for t in (0, 1):
        load(("w", t, 0), w_hbm[t].at[:, pl.ds(0, DEPTH)], w_v.at[t, 0])
    for c in (1, 2):
        for t in (0, 1):
            load(("w", t, c), w_hbm[t].at[:, pl.ds(c * DEPTH, DEPTH)], w_v.at[t, c])
    for c in range(CHUNKS):
        load(("w", 2, c), w_hbm[2].at[:, pl.ds(c * DEPTH, DEPTH)], w_v.at[2, c])

    barrier = pltpu.get_barrier_semaphore()
    for p in partners:
        pl.semaphore_signal(barrier, inc=1, device_id=dev(**p), device_id_type=MESH)

    count = [0]
    started = []

    def send(src, dst, **where):
        i = count[0]
        count[0] += 1
        c = pltpu.make_async_remote_copy(
            src_ref=src, dst_ref=dst, send_sem=ss.at[i], recv_sem=rs.at[i],
            device_id=dev(**where), device_id_type=MESH,
        )
        c.start()
        started.append(c)
        return c

    for s in range(SEQ_LOCAL):
        loads[("x", s)].wait()
        v = x_v[s]
        mean = jnp.mean(v, axis=-1, keepdims=True)
        cen = v - mean
        var = jnp.mean(cen * cen, axis=-1, keepdims=True)
        n_v[pl.ds(s * RES_LOCAL, RES_LOCAL), :] = (cen * lax.rsqrt(var + EPSILON)).astype(BF16)

    def swap(blocks, j):
        return jnp.concatenate([b[:, 64 * j : 64 * j + 64] for b in blocks], axis=1)

    def project(t, c):
        loads[("w", t, c)].wait()
        full = jnp.dot(n_v[...], w_v[t, c], preferred_element_type=F32).astype(BF16)
        blocks = [full[s * RES_LOCAL : (s + 1) * RES_LOCAL] for s in range(SEQ_LOCAL)]
        for j in range(NY):
            send_v[t, c, j] = swap(blocks, j)

    def home(t, c):
        if t == 0:
            return q_v.at[c]
        return (k_v if t == 1 else v_v).at[c, 0]

    def send_y(t, c):
        out = []
        for d in (1, 2, 3):
            out.append(send(send_v.at[t, c, (y + d) % NY], home(t, c).at[y], dy=d))
        return out

    def keep(t, c):
        home(t, c)[y] = send_v[t, c, y]

    def core_swap(t, c):
        b = (k_v if t == 1 else v_v)
        return send(b.at[c, 0], b.at[c, 1], dc=1)

    def starts(row):
        return [sum(w for _, w in row[:g]) for g in range(len(row))]

    def scores(c, g):
        kind, w = SUMS[c][g]
        first = starts(SUMS[c])[g]
        q = q_v[c].reshape(ROWS, DEPTH)
        k = k_v[c].reshape(COLS, DEPTH)[first : first + w]
        r = lax.dot_general(q, k, (((1,), (1,)), ((), ())), preferred_element_type=F32)
        r = (r * SCALE).astype(BF16)
        s_v = sum_refs[c][g][0]
        if kind == "x":
            s_v[...] = r.reshape(NX, NZ, 16, w)
        else:
            for i in range(NX):
                s_v[:, i] = r[i * 128 : (i + 1) * 128].reshape(NZ, 16, w)

    every = pl.ds(0, 16)

    def halves(w):
        first = w // 256 * 128
        return pl.ds(0, first), pl.ds(first, w - first)

    xr, xl, xo = (x + 1) % NX, (x + 3) % NX, (x + 2) % NX
    lo, hi = pl.ds(0, 4), pl.ds(4, 4)

    def wide(v):
        return v.astype(F32)

    class SumX:
        def __init__(self, refs):
            self.s, self.rx1, self.rxl, self.rxr, self.tmp, self.xs, self.zz = refs
            self.half = halves(self.s.shape[-1])

        def start(self):
            s = self.s
            self.r1 = send(s.at[xo, lo], self.rx1.at[0], dx=1)
            self.l1 = send(s.at[xo, hi], self.rx1.at[1], dx=3)
            self.r2 = send(s.at[xr, hi], self.rxl.at[hi], dx=1)
            self.l2 = send(s.at[xl, lo], self.rxr.at[lo], dx=3)

        def relay(self):
            s = self.s
            self.r1.wait_recv()
            self.tmp[0] = (wide(s[xr, lo]) + wide(self.rx1[0])).astype(BF16)
            self.r3 = send(self.tmp.at[0], self.rxl.at[lo], dx=1)
            self.l1.wait_recv()
            self.tmp[1] = (wide(s[xl, hi]) + wide(self.rx1[1])).astype(BF16)
            self.l3 = send(self.tmp.at[1], self.rxr.at[hi], dx=3)

        def total(self):
            for cp in (self.r2, self.l2, self.r3, self.l3):
                cp.wait_recv()
            self.xs[...] = (wide(self.s[x]) + wide(self.rxl[...]) + wide(self.rxr[...])).astype(BF16)
            xs, zz, (a, b) = self.xs, self.zz, self.half
            far = xs.at[(z + 4) % NZ]
            self.h = (send(far.at[every, a], zz.at[0, every, a], dz=2), send(far.at[every, b], zz.at[1, every, b], dz=6))
            self.t = (
                send(xs.at[(z + 3) % NZ], zz.at[2], dz=1),
                send(xs.at[(z + 5) % NZ], zz.at[3], dz=7),
            )
            self.d = (
                send(xs.at[(z + 1) % NZ], zz.at[4], dz=1),
                send(xs.at[(z + 7) % NZ], zz.at[5], dz=7),
            )

        def relay_z(self):
            zz = self.zz
            self.f = []
            for i in (0, 1):
                block = self.xs.at[(z + 2 + 4 * i) % NZ]
                wait_all((self.h[i], self.t[i]))
                near, far = self.half[1 - i], self.half[i]
                zz[6 + i, :, far] = (wide(block[:, far]) + wide(zz[2 + i, :, far]) + wide(zz[i, :, far])).astype(BF16)
                zz[6 + i, :, near] = (wide(block[:, near]) + wide(zz[2 + i, :, near])).astype(BF16)
                self.f.append(send(zz.at[6 + i], zz.at[8 + i], dz=2 + 4 * i))

        def final(self):
            v = wide(self.s[x, z]) + wide(self.rxl[z]) + wide(self.rxr[z])
            wait_all(self.d)
            wait_all(self.f)
            for k in (4, 5, 8, 9):
                v = v + wide(self.zz[k])
            return v

    class SumZ:
        def __init__(self, refs):
            self.s, self.zr, self.zl, self.tz, self.zs, self.rx = refs

        def start(self):
            o = (z + 4) % NZ
            self.r = send(self.s.at[o, pl.ds(0, 2)], self.zr.at[0, pl.ds(0, 2)], dz=1)
            self.l = send(self.s.at[o, pl.ds(2, 2)], self.zl.at[0, pl.ds(2, 2)], dz=7)

        def ring(self, k):
            s, tz = self.s, self.tz
            dr, dl = (z + 5 - k) % NZ, (z + 3 + k) % NZ
            self.r.wait_recv()
            if k == 2:
                tz[0, 0, pl.ds(0, 2)] = (
                    wide(s[dr, pl.ds(0, 2)]) + wide(self.zr[0, pl.ds(0, 2)])
                ).astype(BF16)
                tz[0, 0, pl.ds(2, 2)] = s[dr, pl.ds(2, 2)]
            else:
                tz[k - 2, 0] = (wide(s[dr]) + wide(self.zr[k - 2])).astype(BF16)
            self.r = send(tz.at[k - 2, 0], self.zr.at[k - 1], dz=1)
            self.l.wait_recv()
            if k == 2:
                tz[0, 1, pl.ds(2, 2)] = (
                    wide(s[dl, pl.ds(2, 2)]) + wide(self.zl[0, pl.ds(2, 2)])
                ).astype(BF16)
                tz[0, 1, pl.ds(0, 2)] = s[dl, pl.ds(0, 2)]
            else:
                tz[k - 2, 1] = (wide(s[dl]) + wide(self.zl[k - 2])).astype(BF16)
            self.l = send(tz.at[k - 2, 1], self.zl.at[k - 1], dz=7)

        def total(self):
            self.r.wait_recv()
            self.l.wait_recv()
            self.zs[...] = wide(self.s[z]) + wide(self.zr[3]) + wide(self.zl[3])
            self.x = [send(self.zs.at[(x + d) % NX], self.rx.at[d - 1], dx=d) for d in (2, 1, 3)]

        def final(self):
            wait_all(self.x)
            return self.zs[x] + self.rx[0] + self.rx[1] + self.rx[2]

    class SpreadX:
        def __init__(self, refs):
            (self.p,) = refs
            self.half = halves(self.p.shape[-1])

        def put(self, p):
            self.p[x, z] = p
            mine = self.p.at[x, z]
            self.two = (send(mine, mine, dz=2), send(mine, mine, dz=6))
            self.g = [send(mine, mine, dz=1), send(mine, mine, dz=7)]

        def pass_on(self):
            for i in (0, 1):
                self.two[i].wait_recv()
                block = self.p.at[x, (z + 6 - 4 * i) % NZ]
                half = block.at[every, self.half[i]]
                self.g.append(send(half, half, dz=2 + 4 * i))
                self.g.append(send(block, block, dz=1 + 6 * i))

        def gather(self):
            wait_all(self.g)
            b = self.p.at[x]
            self.ra, self.la = send(b, b, dx=1), send(b, b, dx=3)

        def forward(self):
            self.ra.wait_recv()
            b = self.p.at[xl, lo]
            self.rb = send(b, b, dx=1)
            self.la.wait_recv()
            b = self.p.at[xr, hi]
            self.lb = send(b, b, dx=3)

        def near(self):
            pass

        def done(self):
            wait_all((self.rb, self.lb))

        def rows(self, i):
            return self.p[i].reshape(128, self.p.shape[-1])

    class SpreadZ:
        def __init__(self, refs):
            (self.p,) = refs

        def put(self, p):
            self.p[z, x] = p
            mine = self.p.at[z, x]
            self.g = [send(mine, mine, dx=d) for d in (2, 1, 3)]

        def gather(self, k):
            p = self.p
            if k == 1:
                wait_all(self.g)
                b = p.at[z]
                self.gr, self.gl = send(b, b, dz=1), send(b, b, dz=7)
                return
            zr, zl = (z + k - 1) % NZ, (z + 9 - k) % NZ
            self.gr.wait_recv()
            b = p.at[zl] if k < 4 else p.at[zl, pl.ds(0, 2)]
            self.gr = send(b, b, dz=1)
            self.gl.wait_recv()
            b = p.at[zr] if k < 4 else p.at[zr, pl.ds(2, 2)]
            self.gl = send(b, b, dz=7)

        def near(self):
            wait_all((self.gr, self.gl))

        def done(self):
            pass

        def rows(self, i):
            return self.p[:, i].reshape(128, self.p.shape[-1])

    sums = [
        [(SumX if kind == "x" else SumZ)(refs) for (kind, _), refs in zip(SUMS[c], sum_refs[c])]
        for c in range(CHUNKS)
    ]
    spreads = [
        [
            (SpreadX if kind == "x" else SpreadZ)(refs)
            for (kind, _), refs in zip(SPREADS[c], spread_refs[c])
        ]
        for c in range(CHUNKS)
    ]

    def z_first(c):
        return sorted(range(len(SUMS[c])), key=lambda g: SUMS[c][g][0] == "x")

    def soft(c):
        vals = {g: sums[c][g].final() for g in z_first(c)}
        v = jnp.concatenate([vals[g] for g in range(len(vals))], axis=1)
        e = jnp.exp(v - jnp.max(v, axis=-1, keepdims=True))
        p = (e / jnp.sum(e, axis=-1, keepdims=True)).astype(BF16)
        for g, (_, w) in enumerate(SPREADS[c]):
            first = starts(SPREADS[c])[g]
            spreads[c][g].put(p[:, first : first + w])

    back = {}

    def mix_rows(c, i):
        v = v_v[c].reshape(COLS, DEPTH)
        m = None
        for g, (_, w) in enumerate(SPREADS[c]):
            first = starts(SPREADS[c])[g]
            r = jnp.dot(spreads[c][g].rows(i), v[first : first + w], preferred_element_type=F32)
            m = r if m is None else m + r
        os_v[c, i] = m.astype(BF16)
        d = (i - y + NY) % NY
        base = back[c]

        @pl.when(d == 0)
        def _():
            ob_v[c, y] = os_v[c, i]

        @pl.when(d != 0)
        def _():
            s_, r_ = dev()
            pltpu.make_async_remote_copy(
                src_ref=os_v.at[c, i], dst_ref=ob_v.at[c, y],
                send_sem=ss.at[base + d - 1], recv_sem=rs.at[base + d - 1],
                device_id=(s_, i * 2 + core), device_id_type=MESH,
            ).start()

    def mix_start(c):
        back[c] = count[0]
        count[0] += 3
        ms[c] = [
            pltpu.make_async_remote_copy(
                src_ref=os_v.at[c, (y + d) % NY], dst_ref=ob_v.at[c, y],
                send_sem=ss.at[back[c] + d - 1], recv_sem=rs.at[back[c] + d - 1],
                device_id=dev(dy=d), device_id_type=MESH,
            )
            for d in (1, 2, 3)
        ]
        started.extend(ms[c])

    out_copies = []

    def output(c):
        blocks = [ob_v[c, j] for j in range(NY)]
        for s in range(SEQ_LOCAL):
            m_v[c, pl.ds(s * RES_LOCAL, RES_LOCAL), :] = swap(blocks, s)
        cp = pltpu.make_async_copy(
            m_v.at[c], o_ref.at[:, pl.ds(c * DEPTH, DEPTH)], load_sem.at[13 + c]
        )
        cp.start()
        out_copies.append(cp)

    def wait_all(cps):
        for cp in cps:
            cp.wait_recv()

    qk, vs, kc, vc, ms = {}, {}, {}, {}, {}

    def meet():
        pl.semaphore_wait(barrier, len(partners))

    def first():
        project(1, 0)
        meet()
        qk[0] = send_y(1, 0)
        project(0, 0)
        qk[0] += send_y(0, 0)
        keep(1, 0)
        keep(0, 0)

    def projections(c, ts):
        def go():
            for t in ts:
                project(t, c)
                keep(t, c)
        return go

    def qk_send(c):
        def go():
            qk[c] = send_y(1, c) + send_y(0, c)
        return go

    def k_swap(c):
        def go():
            wait_all(qk[c][:3])
            kc[c] = core_swap(1, c)
        return go

    def score(c):
        def go():
            wait_all(qk[c][3:])
            kc[c].wait_recv()
            for g in z_first(c):
                scores(c, g)
                sums[c][g].start()
        return go

    def add(c, g, what, *args):
        return lambda: getattr(sums[c][g], what)(*args)

    def spread(c, g, what, *args):
        return lambda: getattr(spreads[c][g], what)(*args)

    def softmax(c):
        return lambda: soft(c)

    def v_send(c):
        def go():
            vs[c] = send_y(2, c)
        return go

    def v_swap(c):
        def go():
            wait_all(vs[c])
            vc[c] = core_swap(2, c)
        return go

    def mix_own(c):
        def go():
            for p in spreads[c]:
                p.near()
            vc[c].wait_recv()
            mix_start(c)
            mix_rows(c, x)
        return go

    def mix_near(c):
        def go():
            mix_rows(c, xl)
            mix_rows(c, xr)
        return go

    def mix_far(c):
        def go():
            for p in spreads[c]:
                p.done()
            mix_rows(c, xo)
        return go

    def project_out(c):
        def go():
            wait_all(ms[c])
            output(c)
        return go

    schedule = [
        first, projections(1, (1, 0)), qk_send(1), projections(2, (1, 0)), qk_send(2), projections(0, (2,)),
        k_swap(0), score(0), k_swap(1), add(0, 1, "ring", 2), add(0, 0, "relay"), score(1),
        add(0, 1, "ring", 3), projections(1, (2,)), k_swap(2), add(1, 1, "ring", 2), add(0, 0, "total"),
        v_send(0), add(1, 0, "relay"), score(2), add(0, 1, "ring", 4), add(1, 1, "ring", 3),
        add(0, 0, "relay_z"), add(2, 1, "ring", 2), add(1, 0, "total"), v_swap(0), add(0, 1, "total"),
        add(1, 1, "ring", 4), add(2, 0, "relay"), add(2, 1, "ring", 3), add(1, 0, "relay_z"), softmax(0),
        add(1, 1, "total"), add(2, 0, "total"), add(2, 1, "ring", 4), spread(0, 0, "pass_on"),
        projections(2, (2,)), spread(0, 1, "gather", 1), softmax(1), add(2, 1, "total"), add(2, 0, "relay_z"),
        spread(0, 0, "gather"), spread(0, 1, "gather", 2), spread(1, 1, "gather", 1), spread(1, 0, "pass_on"),
        v_send(1), softmax(2), spread(1, 1, "gather", 2), v_send(2), spread(0, 1, "gather", 3),
        spread(1, 0, "gather"), spread(0, 0, "forward"), spread(2, 1, "gather", 1), spread(2, 0, "pass_on"),
        spread(1, 1, "gather", 3), spread(0, 1, "gather", 4), spread(2, 1, "gather", 2),
        spread(2, 0, "gather"), v_swap(1), mix_own(0), spread(1, 1, "gather", 4), spread(2, 1, "gather", 3),
        mix_near(0), spread(1, 0, "forward"), v_swap(2), spread(2, 1, "gather", 4), mix_own(1), mix_far(0),
        spread(2, 0, "forward"), mix_near(1), mix_far(1), mix_own(2), mix_near(2), mix_far(2), project_out(1),
        project_out(0), project_out(2),
    ]
    for step in schedule:
        step()
    for cp in out_copies:
        cp.wait()
    for cp in started:
        cp.wait_send()


def sum_scratch(kind, w):
    V = pltpu.VMEM
    if kind == "x":
        shapes = [(NX, NZ, 16, w), (2, 4, 16, w), (NZ, 16, w), (NZ, 16, w), (2, 4, 16, w), (NZ, 16, w), (10, 16, w)]
        return [V(s, BF16) for s in shapes]
    shapes = [(NZ, NX, 16, w), (4, NX, 16, w), (4, NX, 16, w), (3, 2, NX, 16, w)]
    return [V(s, BF16) for s in shapes] + [V((n, 16, w), F32) for n in (NX, 3)]


def spread_scratch(kind, w):
    return [pltpu.VMEM((NZ, NX, 16, w) if kind == "z" else (NX, NZ, 16, w), BF16)]


def body(alignment_rows, query_matrix, key_matrix, value_matrix, output_matrix):
    any_spec = pl.BlockSpec(memory_space=pl.ANY)
    hbm_spec = pl.BlockSpec(memory_space=pltpu.HBM)
    V = pltpu.VMEM
    rows = SEQ_LOCAL * RES_LOCAL
    block = (NY, RES_LOCAL, DEPTH)
    scratch = [
        V((SEQ_LOCAL, RES_LOCAL, WIDTH), F32),
        V((rows, WIDTH), BF16),
        V((3, CHUNKS, WIDTH, DEPTH), BF16),
        V((3, CHUNKS) + block, BF16),
        V((CHUNKS,) + block, BF16),
        V((CHUNKS, 2) + block, BF16),
        V((CHUNKS, 2) + block, BF16),
        V((CHUNKS,) + block, BF16),
        V((CHUNKS,) + block, BF16),
        V((CHUNKS, rows, DEPTH), BF16),
        pltpu.SemaphoreType.DMA((16,)),
        pltpu.SemaphoreType.DMA((N_SEMS,)),
        pltpu.SemaphoreType.DMA((N_SEMS,)),
    ]
    for table, make in ((SUMS, sum_scratch), (SPREADS, spread_scratch)):
        for row in table:
            for kind, w in row:
                scratch += make(kind, w)
    inputs = [
        pltpu.with_memory_space_constraint(a, pltpu.HBM)
        for a in (alignment_rows, query_matrix, key_matrix, value_matrix)
    ]
    mixed = pl.pallas_call(
        kernel,
        out_shape=jax.ShapeDtypeStruct((rows, WIDTH), BF16),
        in_specs=[hbm_spec] * 4,
        out_specs=any_spec,
        scratch_shapes=scratch,
        compiler_params=pltpu.CompilerParams(
            collective_id=0, has_side_effects=True, vmem_limit_bytes=34 << 20
        ),
        cost_estimate=pl.CostEstimate(
            flops=5_000_000_000, bytes_accessed=6_000_000, transcendentals=60_000
        ),
    )(*inputs)
    out = jnp.dot(mixed, output_matrix, preferred_element_type=F32)
    return out.reshape(alignment_rows.shape)


def solution(mesh):
    in_specs = (P("seq", "res", None), P(), P(), P(), P())
    out_specs = P("seq", "res", None)
    return jax.shard_map(body, mesh=mesh, in_specs=in_specs, out_specs=out_specs, check_vma=False)
```

```python
import math

import jax
import jax.numpy as jnp
from jax import lax
from jax.experimental import pallas as pl
from jax.experimental.pallas import tpu as pltpu
from jax.sharding import PartitionSpec as P

MESH = pl.DeviceIdType.MESH
F32 = jnp.float32
BF16 = jnp.bfloat16

NZ, NX, NY = 8, 4, 4
CHUNKS = 3
SEQ_LOCAL, RES_LOCAL, WIDTH = 4, 128, 768
ROWS = NY * RES_LOCAL
COLS = 2 * ROWS
DEPTH = 256
SCALE = 1.0 / math.sqrt(64 * 128)
EPSILON = 1e-05
N_SEMS = 194

SUMS = (
    (("x", 512), ("z", 512),),
    (("x", 512), ("z", 512),),
)
SPREADS = (
    (("x", 512), ("z", 512),),
    (("x", 640), ("z", 384),),
)


def kernel(x_hbm, wq_hbm, wk_hbm, wv_hbm, o_ref, *scratch):
    (x_v, n_v, w_v, send_v, q_v, k_v, v_v, os_v, ob_v, m_v, load_sem, ss, rs) = scratch[:13]
    q2, k2, v2, s2, zz2, p2 = scratch[13:19]
    at = 19
    sum_refs, spread_refs = [], []
    for table, store, sizes in ((SUMS, sum_refs, {"x": 7, "z": 6}), (SPREADS, spread_refs, {"x": 1, "z": 1})):
        for row in table:
            store.append([])
            for kind, _ in row:
                store[-1].append(scratch[at : at + sizes[kind]])
                at += sizes[kind]
    s_id, r_id = lax.axis_index("seq"), lax.axis_index("res")
    z, chip_x = s_id // NX, s_id % NX
    y, core = r_id // 2, r_id % 2
    x = (chip_x + y) % NX

    def dev(dz=0, dx=0, dy=0, dc=0):
        return (
            ((z + dz) % NZ) * NX + (chip_x + dx) % NX,
            ((y + dy) % NY) * 2 + (core + dc) % 2,
        )

    partners = (
        [dict(dy=d) for d in (1, 2, 3)]
        + [dict(dc=1)]
        + [dict(dx=d) for d in (1, 2, 3)]
        + [dict(dz=d) for d in (1, 2, 6, 7)]
    )

    loads = {}
    n_load = [0]

    def load(name, src, dst):
        c = pltpu.make_async_copy(src, dst, load_sem.at[n_load[0]])
        n_load[0] += 1
        c.start()
        loads[name] = c

    for s in range(SEQ_LOCAL):
        load(("x", s), x_hbm.at[s], x_v.at[s])
    w_hbm = (wq_hbm, wk_hbm, wv_hbm)
    for t in (0, 1):
        load(("w", t, 0), w_hbm[t].at[:, pl.ds(0, DEPTH)], w_v.at[t, 0])
    for c in (1, 2):
        for t in (0, 1):
            load(("w", t, c), w_hbm[t].at[:, pl.ds(c * DEPTH, DEPTH)], w_v.at[t, c])
    for c in range(CHUNKS):
        load(("w", 2, c), w_hbm[2].at[:, pl.ds(c * DEPTH, DEPTH)], w_v.at[2, c])

    barrier = pltpu.get_barrier_semaphore()
    for p in partners:
        pl.semaphore_signal(barrier, inc=1, device_id=dev(**p), device_id_type=MESH)

    count = [0]
    started = []

    def send(src, dst, **where):
        i = count[0]
        count[0] += 1
        c = pltpu.make_async_remote_copy(
            src_ref=src, dst_ref=dst, send_sem=ss.at[i], recv_sem=rs.at[i],
            device_id=dev(**where), device_id_type=MESH,
        )
        c.start()
        started.append(c)
        return c

    for s in range(SEQ_LOCAL):
        loads[("x", s)].wait()
        v = x_v[s]
        mean = jnp.mean(v, axis=-1, keepdims=True)
        cen = v - mean
        var = jnp.mean(cen * cen, axis=-1, keepdims=True)
        n_v[pl.ds(s * RES_LOCAL, RES_LOCAL), :] = (cen * lax.rsqrt(var + EPSILON)).astype(BF16)

    def swap(blocks, j):
        return jnp.concatenate([b[:, 64 * j : 64 * j + 64] for b in blocks], axis=1)

    def project(t, c):
        loads[("w", t, c)].wait()
        full = jnp.dot(n_v[...], w_v[t, c], preferred_element_type=F32).astype(BF16)
        blocks = [full[s * RES_LOCAL : (s + 1) * RES_LOCAL] for s in range(SEQ_LOCAL)]
        for j in range(NY):
            send_v[t, c, j] = swap(blocks, j)

    def home(t, c):
        if t == 0:
            return q_v.at[c]
        return (k_v if t == 1 else v_v).at[c, 0]

    def send_y(t, c):
        out = []
        for d in (1, 2, 3):
            out.append(send(send_v.at[t, c, (y + d) % NY], home(t, c).at[y], dy=d))
        return out

    def last_home(t):
        return (q2.at[chip_x], k2.at[0, chip_x, y], v2.at[0, chip_x, y])[t]

    def send_x(t):
        return [send(send_v.at[t, 2, (chip_x + d) % NX], last_home(t), dx=d) for d in (1, 2, 3)]

    def keep(t, c):
        if c == 2:
            last_home(t)[...] = send_v[t, 2, chip_x]
        else:
            home(t, c)[y] = send_v[t, c, y]

    def core_swap(t, c):
        b = (k_v if t == 1 else v_v)
        return send(b.at[c, 0], b.at[c, 1], dc=1)

    def starts(row):
        return [sum(w for _, w in row[:g]) for g in range(len(row))]

    def scores(c, g):
        kind, w = SUMS[c][g]
        first = starts(SUMS[c])[g]
        q = q_v[c].reshape(ROWS, DEPTH)
        k = k_v[c].reshape(COLS, DEPTH)[first : first + w]
        r = lax.dot_general(q, k, (((1,), (1,)), ((), ())), preferred_element_type=F32)
        r = (r * SCALE).astype(BF16)
        s_v = sum_refs[c][g][0]
        if kind == "x":
            s_v[...] = r.reshape(NX, NZ, 16, w)
        else:
            for i in range(NX):
                s_v[:, i] = r[i * 128 : (i + 1) * 128].reshape(NZ, 16, w)

    every = pl.ds(0, 16)

    def halves(w):
        first = w // 256 * 128
        return pl.ds(0, first), pl.ds(first, w - first)

    xr, xl, xo = (x + 1) % NX, (x + 3) % NX, (x + 2) % NX
    lo, hi = pl.ds(0, 4), pl.ds(4, 4)

    def wide(v):
        return v.astype(F32)

    class SumX:
        def __init__(self, refs):
            self.s, self.rx1, self.rxl, self.rxr, self.tmp, self.xs, self.zz = refs
            self.half = halves(self.s.shape[-1])

        def start(self):
            s = self.s
            self.r1 = send(s.at[xo, lo], self.rx1.at[0], dx=1)
            self.l1 = send(s.at[xo, hi], self.rx1.at[1], dx=3)
            self.r2 = send(s.at[xr, hi], self.rxl.at[hi], dx=1)
            self.l2 = send(s.at[xl, lo], self.rxr.at[lo], dx=3)

        def relay(self):
            s = self.s
            self.r1.wait_recv()
            self.tmp[0] = (wide(s[xr, lo]) + wide(self.rx1[0])).astype(BF16)
            self.r3 = send(self.tmp.at[0], self.rxl.at[lo], dx=1)
            self.l1.wait_recv()
            self.tmp[1] = (wide(s[xl, hi]) + wide(self.rx1[1])).astype(BF16)
            self.l3 = send(self.tmp.at[1], self.rxr.at[hi], dx=3)

        def total(self):
            for cp in (self.r2, self.l2, self.r3, self.l3):
                cp.wait_recv()
            self.xs[...] = (wide(self.s[x]) + wide(self.rxl[...]) + wide(self.rxr[...])).astype(BF16)
            self.z_start()

        def z_start(self):
            xs, zz, (a, b) = self.xs, self.zz, self.half
            far = xs.at[(z + 4) % NZ]
            self.h = (send(far.at[every, a], zz.at[0, every, a], dz=2), send(far.at[every, b], zz.at[1, every, b], dz=6))
            self.t = (
                send(xs.at[(z + 3) % NZ], zz.at[2], dz=1),
                send(xs.at[(z + 5) % NZ], zz.at[3], dz=7),
            )
            self.d = (
                send(xs.at[(z + 1) % NZ], zz.at[4], dz=1),
                send(xs.at[(z + 7) % NZ], zz.at[5], dz=7),
            )

        def relay_z(self):
            zz = self.zz
            self.f = []
            for i in (0, 1):
                block = self.xs.at[(z + 2 + 4 * i) % NZ]
                wait_all((self.h[i], self.t[i]))
                near, far = self.half[1 - i], self.half[i]
                zz[6 + i, :, far] = (wide(block[:, far]) + wide(zz[2 + i, :, far]) + wide(zz[i, :, far])).astype(BF16)
                zz[6 + i, :, near] = (wide(block[:, near]) + wide(zz[2 + i, :, near])).astype(BF16)
                self.f.append(send(zz.at[6 + i], zz.at[8 + i], dz=2 + 4 * i))

        def final(self):
            v = wide(self.s[x, z]) + wide(self.rxl[z]) + wide(self.rxr[z])
            wait_all(self.d)
            wait_all(self.f)
            for k in (4, 5, 8, 9):
                v = v + wide(self.zz[k])
            return v

    class SumLast(SumX):
        def __init__(self):
            self.xs, self.zz, self.half = s2, zz2, halves(COLS)

        def final(self):
            v = wide(s2[z])
            wait_all(self.d)
            wait_all(self.f)
            for k in (4, 5, 8, 9):
                v = v + wide(zz2[k])
            return v

    class SumZ:
        def __init__(self, refs):
            self.s, self.zr, self.zl, self.tz, self.zs, self.rx = refs

        def start(self):
            o = (z + 4) % NZ
            self.r = send(self.s.at[o, pl.ds(0, 2)], self.zr.at[0, pl.ds(0, 2)], dz=1)
            self.l = send(self.s.at[o, pl.ds(2, 2)], self.zl.at[0, pl.ds(2, 2)], dz=7)

        def ring(self, k):
            s, tz = self.s, self.tz
            dr, dl = (z + 5 - k) % NZ, (z + 3 + k) % NZ
            self.r.wait_recv()
            if k == 2:
                tz[0, 0, pl.ds(0, 2)] = (
                    wide(s[dr, pl.ds(0, 2)]) + wide(self.zr[0, pl.ds(0, 2)])
                ).astype(BF16)
                tz[0, 0, pl.ds(2, 2)] = s[dr, pl.ds(2, 2)]
            else:
                tz[k - 2, 0] = (wide(s[dr]) + wide(self.zr[k - 2])).astype(BF16)
            self.r = send(tz.at[k - 2, 0], self.zr.at[k - 1], dz=1)
            self.l.wait_recv()
            if k == 2:
                tz[0, 1, pl.ds(2, 2)] = (
                    wide(s[dl, pl.ds(2, 2)]) + wide(self.zl[0, pl.ds(2, 2)])
                ).astype(BF16)
                tz[0, 1, pl.ds(0, 2)] = s[dl, pl.ds(0, 2)]
            else:
                tz[k - 2, 1] = (wide(s[dl]) + wide(self.zl[k - 2])).astype(BF16)
            self.l = send(tz.at[k - 2, 1], self.zl.at[k - 1], dz=7)

        def total(self):
            self.r.wait_recv()
            self.l.wait_recv()
            self.zs[...] = wide(self.s[z]) + wide(self.zr[3]) + wide(self.zl[3])
            self.x = [send(self.zs.at[(x + d) % NX], self.rx.at[d - 1], dx=d) for d in (2, 1, 3)]

        def final(self):
            wait_all(self.x)
            return self.zs[x] + self.rx[0] + self.rx[1] + self.rx[2]

    class SpreadX:
        def __init__(self, refs):
            (self.p,) = refs
            self.half = halves(self.p.shape[-1])

        def put(self, p):
            self.p[x, z] = p
            mine = self.p.at[x, z]
            self.two = (send(mine, mine, dz=2), send(mine, mine, dz=6))
            self.g = [send(mine, mine, dz=1), send(mine, mine, dz=7)]

        def pass_on(self):
            for i in (0, 1):
                self.two[i].wait_recv()
                block = self.p.at[x, (z + 6 - 4 * i) % NZ]
                half = block.at[every, self.half[i]]
                self.g.append(send(half, half, dz=2 + 4 * i))
                self.g.append(send(block, block, dz=1 + 6 * i))

        def gather(self):
            wait_all(self.g)
            b = self.p.at[x]
            self.ra, self.la = send(b, b, dx=1), send(b, b, dx=3)

        def forward(self):
            self.ra.wait_recv()
            b = self.p.at[xl, lo]
            self.rb = send(b, b, dx=1)
            self.la.wait_recv()
            b = self.p.at[xr, hi]
            self.lb = send(b, b, dx=3)

        def near(self):
            pass

        def done(self):
            wait_all((self.rb, self.lb))

        def rows(self, i):
            return self.p[i].reshape(128, self.p.shape[-1])

    class SpreadZ:
        def __init__(self, refs):
            (self.p,) = refs

        def put(self, p):
            self.p[z, x] = p
            mine = self.p.at[z, x]
            self.g = [send(mine, mine, dx=d) for d in (2, 1, 3)]

        def gather(self, k):
            p = self.p
            if k == 1:
                wait_all(self.g)
                b = p.at[z]
                self.gr, self.gl = send(b, b, dz=1), send(b, b, dz=7)
                return
            zr, zl = (z + k - 1) % NZ, (z + 9 - k) % NZ
            self.gr.wait_recv()
            b = p.at[zl] if k < 4 else p.at[zl, pl.ds(0, 2)]
            self.gr = send(b, b, dz=1)
            self.gl.wait_recv()
            b = p.at[zr] if k < 4 else p.at[zr, pl.ds(2, 2)]
            self.gl = send(b, b, dz=7)

        def near(self):
            wait_all((self.gr, self.gl))

        def done(self):
            pass

        def rows(self, i):
            return self.p[:, i].reshape(128, self.p.shape[-1])

    sums = [
        [(SumX if kind == "x" else SumZ)(refs) for (kind, _), refs in zip(SUMS[c], sum_refs[c])]
        for c in range(len(SUMS))
    ]
    spreads = [
        [
            (SpreadX if kind == "x" else SpreadZ)(refs)
            for (kind, _), refs in zip(SPREADS[c], spread_refs[c])
        ]
        for c in range(len(SPREADS))
    ]

    def z_first(c):
        return sorted(range(len(SUMS[c])), key=lambda g: SUMS[c][g][0] == "x")

    def soft(c):
        vals = {g: sums[c][g].final() for g in z_first(c)}
        v = jnp.concatenate([vals[g] for g in range(len(vals))], axis=1)
        e = jnp.exp(v - jnp.max(v, axis=-1, keepdims=True))
        p = (e / jnp.sum(e, axis=-1, keepdims=True)).astype(BF16)
        for g, (_, w) in enumerate(SPREADS[c]):
            first = starts(SPREADS[c])[g]
            spreads[c][g].put(p[:, first : first + w])

    back = {}

    def mix_rows(c, i):
        v = v_v[c].reshape(COLS, DEPTH)
        m = None
        for g, (_, w) in enumerate(SPREADS[c]):
            first = starts(SPREADS[c])[g]
            r = jnp.dot(spreads[c][g].rows(i), v[first : first + w], preferred_element_type=F32)
            m = r if m is None else m + r
        os_v[c, i] = m.astype(BF16)
        d = (i - y + NY) % NY
        base = back[c]

        @pl.when(d == 0)
        def _():
            ob_v[c, y] = os_v[c, i]

        @pl.when(d != 0)
        def _():
            s_, r_ = dev()
            pltpu.make_async_remote_copy(
                src_ref=os_v.at[c, i], dst_ref=ob_v.at[c, y],
                send_sem=ss.at[base + d - 1], recv_sem=rs.at[base + d - 1],
                device_id=(s_, i * 2 + core), device_id_type=MESH,
            ).start()

    def mix_start(c):
        back[c] = count[0]
        count[0] += 3
        ms[c] = [
            pltpu.make_async_remote_copy(
                src_ref=os_v.at[c, (y + d) % NY], dst_ref=ob_v.at[c, y],
                send_sem=ss.at[back[c] + d - 1], recv_sem=rs.at[back[c] + d - 1],
                device_id=dev(dy=d), device_id_type=MESH,
            )
            for d in (1, 2, 3)
        ]
        started.extend(ms[c])

    out_copies = []

    def output(c):
        blocks = [ob_v[c, j] for j in range(NY)]
        for s in range(SEQ_LOCAL):
            m_v[c, pl.ds(s * RES_LOCAL, RES_LOCAL), :] = swap(blocks, s)
        cp = pltpu.make_async_copy(
            m_v.at[c], o_ref.at[:, pl.ds(c * DEPTH, DEPTH)], load_sem.at[13 + c]
        )
        cp.start()
        out_copies.append(cp)

    def wait_all(cps):
        for cp in cps:
            cp.wait_recv()

    qk, vs, kc, vc, ms = {}, {}, {}, {}, {}

    def meet():
        pl.semaphore_wait(barrier, len(partners))

    def first():
        project(1, 0)
        meet()
        qk[0] = send_y(1, 0)
        project(0, 0)
        qk[0] += send_y(0, 0)
        keep(1, 0)
        keep(0, 0)

    def projections(c, ts):
        def go():
            for t in ts:
                project(t, c)
                keep(t, c)
        return go

    def qk_send(c):
        def go():
            qk[c] = send_y(1, c) + send_y(0, c)
        return go

    def k_swap(c):
        def go():
            wait_all(qk[c][:3])
            kc[c] = core_swap(1, c)
        return go

    def score(c):
        def go():
            wait_all(qk[c][3:])
            kc[c].wait_recv()
            for g in z_first(c):
                scores(c, g)
                sums[c][g].start()
        return go

    def add(c, g, what, *args):
        return lambda: getattr(sums[c][g], what)(*args)

    def spread(c, g, what, *args):
        return lambda: getattr(spreads[c][g], what)(*args)

    def softmax(c):
        return lambda: soft(c)

    def v_send(c):
        def go():
            vs[c] = send_y(2, c)
        return go

    def v_swap(c):
        def go():
            wait_all(vs[c])
            vc[c] = core_swap(2, c)
        return go

    def mix_own(c):
        def go():
            for p in spreads[c]:
                p.near()
            vc[c].wait_recv()
            mix_start(c)
            mix_rows(c, x)
        return go

    def mix_near(c):
        def go():
            mix_rows(c, xl)
            mix_rows(c, xr)
        return go

    def mix_far(c):
        def go():
            for p in spreads[c]:
                p.done()
            mix_rows(c, xo)
        return go

    def project_out(c):
        def go():
            wait_all(ms[c])
            output(c)
        return go

    last, last_spread, got = SumLast(), SpreadX((p2,)), {}

    def last_send(ts):
        def go():
            for t in ts:
                got[t] = send_x(t)
        return go

    def last_gather(t, k):
        b = k2 if t == 1 else v2

        def go():
            if k == 1:
                wait_all(got[t])
                block = b.at[0, pl.ds(0, 4), y]
                got[t] = (send(block, block, dy=1), send(block, block, dy=3))
            elif k == 2:
                right, left = got[t]
                right.wait_recv()
                block = b.at[0, pl.ds(0, 2), (y + 3) % NY]
                right = send(block, block, dy=1)
                left.wait_recv()
                block = b.at[0, pl.ds(2, 2), (y + 1) % NY]
                got[t] = (right, send(block, block, dy=3))
            else:
                wait_all(got[t])
                got[t] = [send(b.at[0], b.at[1], dc=1)]
        return go

    def last_scores():
        wait_all(got[0])
        wait_all(got[1])
        for half in (0, 1):
            r = None
            for i in range(NX):
                k = k2[half, i].reshape(ROWS, DEPTH)
                d = lax.dot_general(q2[i], k, (((1,), (1,)), ((), ())), preferred_element_type=F32)
                r = d if r is None else r + d
            s2[:, :, pl.ds(half * ROWS, ROWS)] = (r * SCALE).astype(BF16).reshape(NZ, 16, ROWS)
        last.z_start()

    def last_soft():
        v = last.final()
        e = jnp.exp(v - jnp.max(v, axis=-1, keepdims=True))
        last_spread.put((e / jnp.sum(e, axis=-1, keepdims=True)).astype(BF16))

    def last_mix():
        wait_all(last_spread.g)
        wait_all(got[2])
        p = last_spread.rows(x)
        for i in range(NX):
            m = None
            for half in (0, 1):
                v = v2[half, i].reshape(ROWS, DEPTH)
                d = jnp.dot(p[:, half * ROWS : (half + 1) * ROWS], v, preferred_element_type=F32)
                m = d if m is None else m + d
            os_v[2, i] = m.astype(BF16)
        ob_v[2, chip_x] = os_v[2, chip_x]
        ms[2] = [send(os_v.at[2, (chip_x + d) % NX], ob_v.at[2, chip_x], dx=d) for d in (1, 2, 3)]

    schedule = [
        first, projections(2, (1, 0)), projections(2, (2,)), last_send((1, 0)), projections(1, (1, 0)),
        qk_send(1), k_swap(0), last_gather(1, 1), score(0), projections(0, (2,)), v_send(0), last_send((2,)),
        projections(1, (2,)), k_swap(1), add(0, 1, "ring", 2), add(0, 0, "relay"), score(1),
        add(0, 1, "ring", 3), add(1, 1, "ring", 2), last_gather(1, 2), add(0, 0, "total"), last_gather(2, 1),
        add(1, 0, "relay"), add(0, 1, "ring", 4), add(1, 1, "ring", 3), add(0, 0, "relay_z"),
        add(1, 0, "total"), add(0, 1, "total"), last_gather(1, 3), add(1, 1, "ring", 4), add(1, 0, "relay_z"),
        softmax(0), add(1, 1, "total"), last_scores, spread(0, 0, "pass_on"), spread(0, 1, "gather", 1),
        v_swap(0), last_gather(2, 2), softmax(1), last.relay_z, v_send(1), spread(1, 1, "gather", 1),
        spread(0, 0, "gather"), last_gather(2, 3), spread(0, 1, "gather", 2), spread(1, 0, "pass_on"),
        spread(1, 1, "gather", 2), spread(0, 1, "gather", 3), last_soft, spread(1, 0, "gather"),
        spread(1, 1, "gather", 3), spread(0, 1, "gather", 4), spread(0, 0, "forward"), last_spread.pass_on,
        v_swap(1), spread(1, 0, "forward"), spread(1, 1, "gather", 4), mix_own(0), mix_near(0), mix_far(0),
        last_mix, mix_own(1), mix_near(1), mix_far(1), project_out(0), project_out(2), project_out(1),
    ]
    for step in schedule:
        step()
    for cp in out_copies:
        cp.wait()
    for cp in started:
        cp.wait_send()


def sum_scratch(kind, w):
    V = pltpu.VMEM
    if kind == "x":
        shapes = [(NX, NZ, 16, w), (2, 4, 16, w), (NZ, 16, w), (NZ, 16, w), (2, 4, 16, w), (NZ, 16, w), (10, 16, w)]
        return [V(s, BF16) for s in shapes]
    shapes = [(NZ, NX, 16, w), (4, NX, 16, w), (4, NX, 16, w), (3, 2, NX, 16, w)]
    return [V(s, BF16) for s in shapes] + [V((n, 16, w), F32) for n in (NX, 3)]


def spread_scratch(kind, w):
    return [pltpu.VMEM((NZ, NX, 16, w) if kind == "z" else (NX, NZ, 16, w), BF16)]


def body(alignment_rows, query_matrix, key_matrix, value_matrix, output_matrix):
    any_spec = pl.BlockSpec(memory_space=pl.ANY)
    hbm_spec = pl.BlockSpec(memory_space=pltpu.HBM)
    V = pltpu.VMEM
    rows = SEQ_LOCAL * RES_LOCAL
    block = (NY, RES_LOCAL, DEPTH)
    scratch = [
        V((SEQ_LOCAL, RES_LOCAL, WIDTH), F32),
        V((rows, WIDTH), BF16),
        V((3, CHUNKS, WIDTH, DEPTH), BF16),
        V((3, CHUNKS) + block, BF16),
        V((CHUNKS,) + block, BF16),
        V((CHUNKS, 2) + block, BF16),
        V((CHUNKS, 2) + block, BF16),
        V((CHUNKS,) + block, BF16),
        V((CHUNKS,) + block, BF16),
        V((CHUNKS, rows, DEPTH), BF16),
        pltpu.SemaphoreType.DMA((16,)),
        pltpu.SemaphoreType.DMA((N_SEMS,)),
        pltpu.SemaphoreType.DMA((N_SEMS,)),
        V((NX, RES_LOCAL, DEPTH), BF16),
        V((2, NX, NY, RES_LOCAL, DEPTH), BF16),
        V((2, NX, NY, RES_LOCAL, DEPTH), BF16),
        V((NZ, 16, COLS), BF16),
        V((10, 16, COLS), BF16),
        V((NX, NZ, 16, COLS), BF16),
    ]
    for table, make in ((SUMS, sum_scratch), (SPREADS, spread_scratch)):
        for row in table:
            for kind, w in row:
                scratch += make(kind, w)
    inputs = [
        pltpu.with_memory_space_constraint(a, pltpu.HBM)
        for a in (alignment_rows, query_matrix, key_matrix, value_matrix)
    ]
    mixed = pl.pallas_call(
        kernel,
        out_shape=jax.ShapeDtypeStruct((rows, WIDTH), BF16),
        in_specs=[hbm_spec] * 4,
        out_specs=any_spec,
        scratch_shapes=scratch,
        compiler_params=pltpu.CompilerParams(
            collective_id=0, has_side_effects=True, vmem_limit_bytes=34 << 20
        ),
        cost_estimate=pl.CostEstimate(
            flops=5_000_000_000, bytes_accessed=6_000_000, transcendentals=60_000
        ),
    )(*inputs)
    out = jnp.dot(mixed, output_matrix, preferred_element_type=F32)
    return out.reshape(alignment_rows.shape)


def solution(mesh):
    in_specs = (P("seq", "res", None), P(), P(), P(), P())
    out_specs = P("seq", "res", None)
    return jax.shard_map(body, mesh=mesh, in_specs=in_specs, out_specs=out_specs, check_vma=False)
```

```python
import math

import jax
import jax.numpy as jnp
from jax import lax
from jax.experimental import pallas as pl
from jax.experimental.pallas import tpu as pltpu
from jax.sharding import PartitionSpec as P

MESH = pl.DeviceIdType.MESH
F32 = jnp.float32
BF16 = jnp.bfloat16

NZ, NX, NY = 8, 4, 4
CHUNKS = 3
SEQ_LOCAL, RES_LOCAL, WIDTH = 4, 128, 768
ROWS = NY * RES_LOCAL
COLS = 2 * ROWS
DEPTH = 256
SCALE = 1.0 / math.sqrt(64 * 128)
EPSILON = 1e-05
N_SEMS = 194

SUMS = (
    (("x", 512), ("z", 512),),
    (("x", 512), ("z", 512),),
)
SPREADS = (
    (("x", 768), ("z", 256),),
    (("x", 768), ("z", 256),),
)


def kernel(x_hbm, wq_hbm, wk_hbm, wv_hbm, o_ref, *scratch):
    (x_v, n_v, w_v, send_v, q_v, k_v, v_v, os_v, ob_v, m_v, load_sem, ss, rs) = scratch[:13]
    q2, k2, v2, s2, zz2, p2 = scratch[13:19]
    at = 19
    sum_refs, spread_refs = [], []
    for table, store, sizes in ((SUMS, sum_refs, {"x": 7, "z": 6}), (SPREADS, spread_refs, {"x": 1, "z": 1})):
        for row in table:
            store.append([])
            for kind, _ in row:
                store[-1].append(scratch[at : at + sizes[kind]])
                at += sizes[kind]
    s_id, r_id = lax.axis_index("seq"), lax.axis_index("res")
    z, chip_x = s_id // NX, s_id % NX
    y, core = r_id // 2, r_id % 2
    x = (chip_x + y) % NX

    def dev(dz=0, dx=0, dy=0, dc=0):
        return (
            ((z + dz) % NZ) * NX + (chip_x + dx) % NX,
            ((y + dy) % NY) * 2 + (core + dc) % 2,
        )

    partners = (
        [dict(dy=d) for d in (1, 2, 3)]
        + [dict(dc=1)]
        + [dict(dx=d) for d in (1, 2, 3)]
        + [dict(dz=d) for d in (1, 2, 6, 7)]
    )

    loads = {}
    n_load = [0]

    def load(name, src, dst):
        c = pltpu.make_async_copy(src, dst, load_sem.at[n_load[0]])
        n_load[0] += 1
        c.start()
        loads[name] = c

    for s in range(SEQ_LOCAL):
        load(("x", s), x_hbm.at[s], x_v.at[s])
    w_hbm = (wq_hbm, wk_hbm, wv_hbm)
    for t in (0, 1):
        load(("w", t, 0), w_hbm[t].at[:, pl.ds(0, DEPTH)], w_v.at[t, 0])
    for c in (1, 2):
        for t in (0, 1):
            load(("w", t, c), w_hbm[t].at[:, pl.ds(c * DEPTH, DEPTH)], w_v.at[t, c])
    for c in range(CHUNKS):
        load(("w", 2, c), w_hbm[2].at[:, pl.ds(c * DEPTH, DEPTH)], w_v.at[2, c])

    barrier = pltpu.get_barrier_semaphore()
    for p in partners:
        pl.semaphore_signal(barrier, inc=1, device_id=dev(**p), device_id_type=MESH)

    count = [0]
    started = []

    def send(src, dst, **where):
        i = count[0]
        count[0] += 1
        c = pltpu.make_async_remote_copy(
            src_ref=src, dst_ref=dst, send_sem=ss.at[i], recv_sem=rs.at[i],
            device_id=dev(**where), device_id_type=MESH,
        )
        c.start()
        started.append(c)
        return c

    for s in range(SEQ_LOCAL):
        loads[("x", s)].wait()
        v = x_v[s]
        mean = jnp.mean(v, axis=-1, keepdims=True)
        cen = v - mean
        var = jnp.mean(cen * cen, axis=-1, keepdims=True)
        n_v[pl.ds(s * RES_LOCAL, RES_LOCAL), :] = (cen * lax.rsqrt(var + EPSILON)).astype(BF16)

    def swap(blocks, j):
        return jnp.concatenate([b[:, 64 * j : 64 * j + 64] for b in blocks], axis=1)

    def project(t, c):
        loads[("w", t, c)].wait()
        full = jnp.dot(n_v[...], w_v[t, c], preferred_element_type=F32).astype(BF16)
        blocks = [full[s * RES_LOCAL : (s + 1) * RES_LOCAL] for s in range(SEQ_LOCAL)]
        for j in range(NY):
            send_v[t, c, j] = swap(blocks, j)

    def home(t, c):
        if t == 0:
            return q_v.at[c]
        return (k_v if t == 1 else v_v).at[c, 0]

    def send_y(t, c):
        out = []
        for d in (1, 2, 3):
            out.append(send(send_v.at[t, c, (y + d) % NY], home(t, c).at[y], dy=d))
        return out

    def last_home(t):
        return (q2.at[chip_x], k2.at[0, chip_x, y], v2.at[0, chip_x, y])[t]

    def send_x(t):
        return [send(send_v.at[t, 2, (chip_x + d) % NX], last_home(t), dx=d) for d in (1, 2, 3)]

    def keep(t, c):
        if c == 2:
            last_home(t)[...] = send_v[t, 2, chip_x]
        else:
            home(t, c)[y] = send_v[t, c, y]

    def core_swap(t, c):
        b = (k_v if t == 1 else v_v)
        return send(b.at[c, 0], b.at[c, 1], dc=1)

    def starts(row):
        return [sum(w for _, w in row[:g]) for g in range(len(row))]

    def scores(c, g):
        kind, w = SUMS[c][g]
        first = starts(SUMS[c])[g]
        q = q_v[c].reshape(ROWS, DEPTH)
        k = k_v[c].reshape(COLS, DEPTH)[first : first + w]
        r = lax.dot_general(q, k, (((1,), (1,)), ((), ())), preferred_element_type=F32)
        r = (r * SCALE).astype(BF16)
        s_v = sum_refs[c][g][0]
        if kind == "x":
            s_v[...] = r.reshape(NX, NZ, 16, w)
        else:
            for i in range(NX):
                s_v[:, i] = r[i * 128 : (i + 1) * 128].reshape(NZ, 16, w)

    every = pl.ds(0, 16)

    def halves(w):
        first = w // 256 * 128
        return pl.ds(0, first), pl.ds(first, w - first)

    xr, xl, xo = (x + 1) % NX, (x + 3) % NX, (x + 2) % NX
    lo, hi = pl.ds(0, 4), pl.ds(4, 4)

    def wide(v):
        return v.astype(F32)

    class SumX:
        def __init__(self, refs):
            self.s, self.rx1, self.rxl, self.rxr, self.tmp, self.xs, self.zz = refs
            self.half = halves(self.s.shape[-1])

        def start(self):
            s = self.s
            self.r1 = send(s.at[xo, lo], self.rx1.at[0], dx=1)
            self.l1 = send(s.at[xo, hi], self.rx1.at[1], dx=3)
            self.r2 = send(s.at[xr, hi], self.rxl.at[hi], dx=1)
            self.l2 = send(s.at[xl, lo], self.rxr.at[lo], dx=3)

        def relay(self):
            s = self.s
            self.r1.wait_recv()
            self.tmp[0] = (wide(s[xr, lo]) + wide(self.rx1[0])).astype(BF16)
            self.r3 = send(self.tmp.at[0], self.rxl.at[lo], dx=1)
            self.l1.wait_recv()
            self.tmp[1] = (wide(s[xl, hi]) + wide(self.rx1[1])).astype(BF16)
            self.l3 = send(self.tmp.at[1], self.rxr.at[hi], dx=3)

        def total(self):
            for cp in (self.r2, self.l2, self.r3, self.l3):
                cp.wait_recv()
            self.xs[...] = (wide(self.s[x]) + wide(self.rxl[...]) + wide(self.rxr[...])).astype(BF16)
            self.z_start()

        def z_start(self):
            xs, zz, (a, b) = self.xs, self.zz, self.half
            far = xs.at[(z + 4) % NZ]
            self.h = (send(far.at[every, a], zz.at[0, every, a], dz=2), send(far.at[every, b], zz.at[1, every, b], dz=6))
            self.t = (
                send(xs.at[(z + 3) % NZ], zz.at[2], dz=1),
                send(xs.at[(z + 5) % NZ], zz.at[3], dz=7),
            )
            self.d = (
                send(xs.at[(z + 1) % NZ], zz.at[4], dz=1),
                send(xs.at[(z + 7) % NZ], zz.at[5], dz=7),
            )

        def relay_z(self):
            zz = self.zz
            self.f = []
            for i in (0, 1):
                block = self.xs.at[(z + 2 + 4 * i) % NZ]
                wait_all((self.h[i], self.t[i]))
                near, far = self.half[1 - i], self.half[i]
                zz[6 + i, :, far] = (wide(block[:, far]) + wide(zz[2 + i, :, far]) + wide(zz[i, :, far])).astype(BF16)
                zz[6 + i, :, near] = (wide(block[:, near]) + wide(zz[2 + i, :, near])).astype(BF16)
                self.f.append(send(zz.at[6 + i], zz.at[8 + i], dz=2 + 4 * i))

        def final(self):
            v = wide(self.s[x, z]) + wide(self.rxl[z]) + wide(self.rxr[z])
            wait_all(self.d)
            wait_all(self.f)
            for k in (4, 5, 8, 9):
                v = v + wide(self.zz[k])
            return v

    class SumLast(SumX):
        def __init__(self):
            self.xs, self.zz, self.half = s2, zz2, halves(COLS)

        def final(self):
            v = wide(s2[z])
            wait_all(self.d)
            wait_all(self.f)
            for k in (4, 5, 8, 9):
                v = v + wide(zz2[k])
            return v

    class SumZ:
        def __init__(self, refs):
            self.s, self.zr, self.zl, self.tz, self.zs, self.rx = refs

        def start(self):
            o = (z + 4) % NZ
            self.r = send(self.s.at[o, pl.ds(0, 2)], self.zr.at[0, pl.ds(0, 2)], dz=1)
            self.l = send(self.s.at[o, pl.ds(2, 2)], self.zl.at[0, pl.ds(2, 2)], dz=7)

        def ring(self, k):
            s, tz = self.s, self.tz
            dr, dl = (z + 5 - k) % NZ, (z + 3 + k) % NZ
            self.r.wait_recv()
            if k == 2:
                tz[0, 0, pl.ds(0, 2)] = (
                    wide(s[dr, pl.ds(0, 2)]) + wide(self.zr[0, pl.ds(0, 2)])
                ).astype(BF16)
                tz[0, 0, pl.ds(2, 2)] = s[dr, pl.ds(2, 2)]
            else:
                tz[k - 2, 0] = (wide(s[dr]) + wide(self.zr[k - 2])).astype(BF16)
            self.r = send(tz.at[k - 2, 0], self.zr.at[k - 1], dz=1)
            self.l.wait_recv()
            if k == 2:
                tz[0, 1, pl.ds(2, 2)] = (
                    wide(s[dl, pl.ds(2, 2)]) + wide(self.zl[0, pl.ds(2, 2)])
                ).astype(BF16)
                tz[0, 1, pl.ds(0, 2)] = s[dl, pl.ds(0, 2)]
            else:
                tz[k - 2, 1] = (wide(s[dl]) + wide(self.zl[k - 2])).astype(BF16)
            self.l = send(tz.at[k - 2, 1], self.zl.at[k - 1], dz=7)

        def total(self):
            self.r.wait_recv()
            self.l.wait_recv()
            self.zs[...] = wide(self.s[z]) + wide(self.zr[3]) + wide(self.zl[3])
            self.x = [send(self.zs.at[(x + d) % NX], self.rx.at[d - 1], dx=d) for d in (2, 1, 3)]

        def final(self):
            wait_all(self.x)
            return self.zs[x] + self.rx[0] + self.rx[1] + self.rx[2]

    class SpreadX:
        def __init__(self, refs):
            (self.p,) = refs
            self.half = halves(self.p.shape[-1])

        def put(self, p):
            self.p[x, z] = p
            mine = self.p.at[x, z]
            self.two = (send(mine, mine, dz=2), send(mine, mine, dz=6))
            self.g = [send(mine, mine, dz=1), send(mine, mine, dz=7)]

        def pass_on(self):
            for i in (0, 1):
                self.two[i].wait_recv()
                block = self.p.at[x, (z + 6 - 4 * i) % NZ]
                half = block.at[every, self.half[i]]
                self.g.append(send(half, half, dz=2 + 4 * i))
                self.g.append(send(block, block, dz=1 + 6 * i))

        def gather(self):
            wait_all(self.g)
            b = self.p.at[x]
            self.ra, self.la = send(b, b, dx=1), send(b, b, dx=3)

        def forward(self):
            self.ra.wait_recv()
            b = self.p.at[xl, lo]
            self.rb = send(b, b, dx=1)
            self.la.wait_recv()
            b = self.p.at[xr, hi]
            self.lb = send(b, b, dx=3)

        def near(self):
            pass

        def done(self):
            wait_all((self.rb, self.lb))

        def rows(self, i):
            return self.p[i].reshape(128, self.p.shape[-1])

    class SpreadZ:
        def __init__(self, refs):
            (self.p,) = refs

        def put(self, p):
            self.p[z, x] = p
            mine = self.p.at[z, x]
            self.g = [send(mine, mine, dx=d) for d in (2, 1, 3)]

        def gather(self, k):
            p = self.p
            if k == 1:
                wait_all(self.g)
                b = p.at[z]
                self.gr, self.gl = send(b, b, dz=1), send(b, b, dz=7)
                return
            zr, zl = (z + k - 1) % NZ, (z + 9 - k) % NZ
            self.gr.wait_recv()
            b = p.at[zl] if k < 4 else p.at[zl, pl.ds(0, 2)]
            self.gr = send(b, b, dz=1)
            self.gl.wait_recv()
            b = p.at[zr] if k < 4 else p.at[zr, pl.ds(2, 2)]
            self.gl = send(b, b, dz=7)

        def near(self):
            wait_all((self.gr, self.gl))

        def done(self):
            pass

        def rows(self, i):
            return self.p[:, i].reshape(128, self.p.shape[-1])

    sums = [
        [(SumX if kind == "x" else SumZ)(refs) for (kind, _), refs in zip(SUMS[c], sum_refs[c])]
        for c in range(len(SUMS))
    ]
    spreads = [
        [
            (SpreadX if kind == "x" else SpreadZ)(refs)
            for (kind, _), refs in zip(SPREADS[c], spread_refs[c])
        ]
        for c in range(len(SPREADS))
    ]

    def z_first(c):
        return sorted(range(len(SUMS[c])), key=lambda g: SUMS[c][g][0] == "x")

    def soft(c):
        vals = {g: sums[c][g].final() for g in z_first(c)}
        v = jnp.concatenate([vals[g] for g in range(len(vals))], axis=1)
        e = jnp.exp(v - jnp.max(v, axis=-1, keepdims=True))
        p = (e / jnp.sum(e, axis=-1, keepdims=True)).astype(BF16)
        for g, (_, w) in enumerate(SPREADS[c]):
            first = starts(SPREADS[c])[g]
            spreads[c][g].put(p[:, first : first + w])

    back = {}

    def mix_rows(c, i):
        v = v_v[c].reshape(COLS, DEPTH)
        m = None
        for g, (_, w) in enumerate(SPREADS[c]):
            first = starts(SPREADS[c])[g]
            r = jnp.dot(spreads[c][g].rows(i), v[first : first + w], preferred_element_type=F32)
            m = r if m is None else m + r
        os_v[c, i] = m.astype(BF16)
        d = (i - y + NY) % NY
        base = back[c]

        @pl.when(d == 0)
        def _():
            ob_v[c, y] = os_v[c, i]

        @pl.when(d != 0)
        def _():
            s_, r_ = dev()
            pltpu.make_async_remote_copy(
                src_ref=os_v.at[c, i], dst_ref=ob_v.at[c, y],
                send_sem=ss.at[base + d - 1], recv_sem=rs.at[base + d - 1],
                device_id=(s_, i * 2 + core), device_id_type=MESH,
            ).start()

    def mix_start(c):
        back[c] = count[0]
        count[0] += 3
        ms[c] = [
            pltpu.make_async_remote_copy(
                src_ref=os_v.at[c, (y + d) % NY], dst_ref=ob_v.at[c, y],
                send_sem=ss.at[back[c] + d - 1], recv_sem=rs.at[back[c] + d - 1],
                device_id=dev(dy=d), device_id_type=MESH,
            )
            for d in (1, 2, 3)
        ]
        started.extend(ms[c])

    out_copies = []

    def output(c):
        blocks = [ob_v[c, j] for j in range(NY)]
        for s in range(SEQ_LOCAL):
            m_v[c, pl.ds(s * RES_LOCAL, RES_LOCAL), :] = swap(blocks, s)
        cp = pltpu.make_async_copy(
            m_v.at[c], o_ref.at[:, pl.ds(c * DEPTH, DEPTH)], load_sem.at[13 + c]
        )
        cp.start()
        out_copies.append(cp)

    def wait_all(cps):
        for cp in cps:
            cp.wait_recv()

    qk, vs, kc, vc, ms = {}, {}, {}, {}, {}

    def meet():
        pl.semaphore_wait(barrier, len(partners))

    def first():
        project(1, 0)
        meet()
        qk[0] = send_y(1, 0)
        project(0, 0)
        qk[0] += send_y(0, 0)
        keep(1, 0)
        keep(0, 0)

    def projections(c, ts):
        def go():
            for t in ts:
                project(t, c)
                keep(t, c)
        return go

    def qk_send(c):
        def go():
            qk[c] = send_y(1, c) + send_y(0, c)
        return go

    def k_swap(c):
        def go():
            wait_all(qk[c][:3])
            kc[c] = core_swap(1, c)
        return go

    def score(c):
        def go():
            wait_all(qk[c][3:])
            kc[c].wait_recv()
            for g in z_first(c):
                scores(c, g)
                sums[c][g].start()
        return go

    def add(c, g, what, *args):
        return lambda: getattr(sums[c][g], what)(*args)

    def spread(c, g, what, *args):
        return lambda: getattr(spreads[c][g], what)(*args)

    def softmax(c):
        return lambda: soft(c)

    def v_send(c):
        def go():
            vs[c] = send_y(2, c)
        return go

    def v_swap(c):
        def go():
            wait_all(vs[c])
            vc[c] = core_swap(2, c)
        return go

    def mix_own(c):
        def go():
            for p in spreads[c]:
                p.near()
            vc[c].wait_recv()
            mix_start(c)
            mix_rows(c, x)
        return go

    def mix_near(c):
        def go():
            mix_rows(c, xl)
            mix_rows(c, xr)
        return go

    def mix_far(c):
        def go():
            for p in spreads[c]:
                p.done()
            mix_rows(c, xo)
        return go

    def project_out(c):
        def go():
            wait_all(ms[c])
            output(c)
        return go

    last, last_spread, got = SumLast(), SpreadX((p2,)), {}

    def last_send(ts):
        def go():
            for t in ts:
                got[t] = send_x(t)
        return go

    def last_gather(t, k):
        b = k2 if t == 1 else v2

        def go():
            if k == 1:
                wait_all(got[t])
                block = b.at[0, pl.ds(0, 4), y]
                got[t] = (send(block, block, dy=1), send(block, block, dy=3))
            elif k == 2:
                right, left = got[t]
                right.wait_recv()
                block = b.at[0, pl.ds(0, 2), (y + 3) % NY]
                right = send(block, block, dy=1)
                left.wait_recv()
                block = b.at[0, pl.ds(2, 2), (y + 1) % NY]
                got[t] = (right, send(block, block, dy=3))
            else:
                wait_all(got[t])
                got[t] = [send(b.at[0], b.at[1], dc=1)]
        return go

    def last_scores():
        wait_all(got[0])
        wait_all(got[1])
        for half in (0, 1):
            r = None
            for i in range(NX):
                k = k2[half, i].reshape(ROWS, DEPTH)
                d = lax.dot_general(q2[i], k, (((1,), (1,)), ((), ())), preferred_element_type=F32)
                r = d if r is None else r + d
            s2[:, :, pl.ds(half * ROWS, ROWS)] = (r * SCALE).astype(BF16).reshape(NZ, 16, ROWS)
        last.z_start()

    def last_soft():
        v = last.final()
        e = jnp.exp(v - jnp.max(v, axis=-1, keepdims=True))
        last_spread.put((e / jnp.sum(e, axis=-1, keepdims=True)).astype(BF16))

    def last_mix():
        wait_all(last_spread.g)
        wait_all(got[2])
        p = last_spread.rows(x)
        for i in range(NX):
            m = None
            for half in (0, 1):
                v = v2[half, i].reshape(ROWS, DEPTH)
                d = jnp.dot(p[:, half * ROWS : (half + 1) * ROWS], v, preferred_element_type=F32)
                m = d if m is None else m + d
            os_v[2, i] = m.astype(BF16)
        ob_v[2, chip_x] = os_v[2, chip_x]
        ms[2] = [send(os_v.at[2, (chip_x + d) % NX], ob_v.at[2, chip_x], dx=d) for d in (1, 2, 3)]

    schedule = [
        first, projections(1, (1, 0)), projections(2, (1, 0)), last_send((1, 0)), projections(2, (2,)),
        qk_send(1), k_swap(0), score(0), last_gather(1, 1), k_swap(1), add(0, 1, "ring", 2),
        add(0, 0, "relay"), projections(1, (2,)), score(1), add(0, 1, "ring", 3), add(1, 1, "ring", 2),
        add(1, 0, "relay"), add(0, 0, "total"), last_gather(1, 2), last_send((2,)), projections(0, (2,)),
        add(0, 1, "ring", 4), v_send(0), add(1, 1, "ring", 3), add(0, 0, "relay_z"), add(1, 0, "total"),
        add(0, 1, "total"), last_gather(1, 3), add(1, 1, "ring", 4), add(1, 0, "relay_z"), last_gather(2, 1),
        softmax(0), add(1, 1, "total"), last_scores, spread(0, 1, "gather", 1), spread(0, 0, "pass_on"),
        softmax(1), last_gather(2, 2), last.relay_z, spread(0, 0, "gather"), spread(0, 1, "gather", 2),
        spread(1, 1, "gather", 1), spread(1, 0, "pass_on"), spread(0, 1, "gather", 3), v_send(1),
        last_gather(2, 3), spread(1, 1, "gather", 2), last_soft, spread(1, 0, "gather"), v_swap(0),
        spread(1, 1, "gather", 3), spread(0, 0, "forward"), spread(0, 1, "gather", 4), last_spread.pass_on,
        v_swap(1), spread(1, 1, "gather", 4), mix_own(0), spread(1, 0, "forward"), mix_near(0), last_mix,
        mix_far(0), mix_own(1), mix_near(1), mix_far(1), project_out(0), project_out(2), project_out(1),
    ]
    for step in schedule:
        step()
    for cp in out_copies:
        cp.wait()
    for cp in started:
        cp.wait_send()


def sum_scratch(kind, w):
    V = pltpu.VMEM
    if kind == "x":
        shapes = [(NX, NZ, 16, w), (2, 4, 16, w), (NZ, 16, w), (NZ, 16, w), (2, 4, 16, w), (NZ, 16, w), (10, 16, w)]
        return [V(s, BF16) for s in shapes]
    shapes = [(NZ, NX, 16, w), (4, NX, 16, w), (4, NX, 16, w), (3, 2, NX, 16, w)]
    return [V(s, BF16) for s in shapes] + [V((n, 16, w), F32) for n in (NX, 3)]


def spread_scratch(kind, w):
    return [pltpu.VMEM((NZ, NX, 16, w) if kind == "z" else (NX, NZ, 16, w), BF16)]


def body(alignment_rows, query_matrix, key_matrix, value_matrix, output_matrix):
    any_spec = pl.BlockSpec(memory_space=pl.ANY)
    hbm_spec = pl.BlockSpec(memory_space=pltpu.HBM)
    V = pltpu.VMEM
    rows = SEQ_LOCAL * RES_LOCAL
    block = (NY, RES_LOCAL, DEPTH)
    scratch = [
        V((SEQ_LOCAL, RES_LOCAL, WIDTH), F32),
        V((rows, WIDTH), BF16),
        V((3, CHUNKS, WIDTH, DEPTH), BF16),
        V((3, CHUNKS) + block, BF16),
        V((CHUNKS,) + block, BF16),
        V((CHUNKS, 2) + block, BF16),
        V((CHUNKS, 2) + block, BF16),
        V((CHUNKS,) + block, BF16),
        V((CHUNKS,) + block, BF16),
        V((CHUNKS, rows, DEPTH), BF16),
        pltpu.SemaphoreType.DMA((16,)),
        pltpu.SemaphoreType.DMA((N_SEMS,)),
        pltpu.SemaphoreType.DMA((N_SEMS,)),
        V((NX, RES_LOCAL, DEPTH), BF16),
        V((2, NX, NY, RES_LOCAL, DEPTH), BF16),
        V((2, NX, NY, RES_LOCAL, DEPTH), BF16),
        V((NZ, 16, COLS), BF16),
        V((10, 16, COLS), BF16),
        V((NX, NZ, 16, COLS), BF16),
    ]
    for table, make in ((SUMS, sum_scratch), (SPREADS, spread_scratch)):
        for row in table:
            for kind, w in row:
                scratch += make(kind, w)
    inputs = [
        pltpu.with_memory_space_constraint(a, pltpu.HBM)
        for a in (alignment_rows, query_matrix, key_matrix, value_matrix)
    ]
    mixed = pl.pallas_call(
        kernel,
        out_shape=jax.ShapeDtypeStruct((rows, WIDTH), BF16),
        in_specs=[hbm_spec] * 4,
        out_specs=any_spec,
        scratch_shapes=scratch,
        compiler_params=pltpu.CompilerParams(
            collective_id=0, has_side_effects=True, vmem_limit_bytes=34 << 20
        ),
        cost_estimate=pl.CostEstimate(
            flops=5_000_000_000, bytes_accessed=6_000_000, transcendentals=60_000
        ),
    )(*inputs)
    out = jnp.dot(mixed, output_matrix, preferred_element_type=F32)
    return out.reshape(alignment_rows.shape)


def solution(mesh):
    in_specs = (P("seq", "res", None), P(), P(), P(), P())
    out_specs = P("seq", "res", None)
    return jax.shard_map(body, mesh=mesh, in_specs=in_specs, out_specs=out_specs, check_vma=False)
```
